256 devices in a mesh: sp: 32 (over y, z_lo, x), op: 8 (over z_hi, core).
Axes of the slice: x: 4, y: 4, z: 8 (z_hi: 4, z_lo: 2; z = z_hi * 2 + z_lo), core: 2. Of those that a mesh axis runs over, the one named last changes fastest.
Arguments:
- amplitudes: bfloat16 [256, 1408, 1408], P('op', 'sp'), may hold values from -6 to 6
- window_coef: bfloat16 [12, 1408], replicated, may hold values from -0.4375 to 0.4375
- virtual_coef: bfloat16 [2048, 1408], P(None, 'sp'), may hold values from -0.15625 to 0.15625
- integrals: bfloat16 [24576, 24576], P('sp', 'op'), may hold values from -0.0390625 to 0.0390625
- block_mask: int32 [96, 96], P('sp', 'op'), may hold values 0 or 1
Outputs:
- ladder_out: bfloat16 [256, 1408, 1408], P('op', 'sp')
The draws below stay inside these ranges and needn't reach their ends.
All inputs are finite; a program needn't handle non-finite values. No bound on the sum of `block_mask` on one device may be relied on, other than what follows from the above.
Results may differ from the reference program's by a relative error of at most 0.013.
Values may be sent and summed in bfloat16 or wider, within the bound.
No kernel may reach another device: no remote copies, remote signals or barrier semaphores. Data moves between devices by JAX's collectives and lax.ppermute only.
A program may use at most 128 MiB of HBM per device.

```python
import jax
import jax.numpy as jnp
from jax import lax

NAO = 2048
NV = 1408
NUW = 12
BLK = 256
PAIRS = 256
NPAIR = 24576


def place_ends(result, key, least, largest):
    shape = result.shape
    place = [jax.random.randint(jax.random.fold_in(key, axis), (), 0, shape[axis]) for axis in range(len(shape))]
    result = result.at[tuple(place)].set(least)
    longest = shape.index(max(shape))
    place[longest] = (place[longest] + 1) % shape[longest]
    return result.at[tuple(place)].set(largest)


def steps_of(stream_key, shape, pieces, low, top_value):
    level = 1.0
    for position, blocks in pieces:
        steps = jax.random.uniform(jax.random.fold_in(jax.random.fold_in(stream_key, 6), position), (blocks,), jnp.float32, low / len(pieces), top_value / len(pieces))
        level = level * jnp.repeat(jnp.exp(steps), shape[position] // blocks).reshape((-1,) + (1,) * (len(shape) - 1 - position))
    return level


def centred(stream_key, shape, spread, bound, cuts=(), kind=jnp.bfloat16):
    level = steps_of(stream_key, shape, cuts, -0.22, 0.18) if cuts else 1.0
    array = jax.random.normal(stream_key, shape, jnp.float32) * spread * level
    return jnp.minimum(jnp.maximum(array, -bound), bound).astype(kind)


def setup_inputs(seed: int = 0) -> dict:
    keys = jax.random.split(jax.random.key(seed), 6)
    return {
        "amplitudes": centred(keys[0], (PAIRS, NV, NV), 1.0, 6.0, ((0, 8), (1, 32))),
        "window_coef": centred(keys[1], (NUW, NV), (NUW * 16) ** -0.5, 0.4375),
        "virtual_coef": centred(keys[2], (NAO, NV), NV ** -0.5, 0.15625, ((1, 32),)),
        "integrals": centred(keys[3], (NPAIR, NPAIR), NPAIR ** -0.5, 0.0390625, ((0, 32), (1, 8))),
        "block_mask": place_ends((jax.random.randint(keys[4], (NPAIR // BLK, NPAIR // BLK), 0, 4) < 3).astype(jnp.int32), jax.random.fold_in(keys[4], 1), 0, 1),
    }


def reference(amplitudes, window_coef, virtual_coef, integrals, block_mask):
    win = window_coef.astype(jnp.float32)
    coef = virtual_coef.astype(jnp.float32)
    half = jnp.einsum("pab,nb->pan", amplitudes.astype(jnp.float32), win).astype(jnp.bfloat16)
    ao_amp = jnp.einsum("ma,pan->pmn", coef, half.astype(jnp.float32)).astype(jnp.bfloat16)
    ao_amp = ao_amp.reshape(PAIRS, NPAIR)
    blocks = NPAIR // BLK

    def one_block(index, total):
        start = (index * BLK).astype(jnp.int32)
        rows = lax.dynamic_slice_in_dim(integrals, start, BLK, 0)
        keep = lax.dynamic_index_in_dim(block_mask, index, 0, keepdims=False)
        keep = jnp.repeat(keep, BLK, total_repeat_length=NPAIR).astype(integrals.dtype)
        rows = rows * keep[None, :]
        left = lax.dynamic_slice_in_dim(ao_amp, start, BLK, 1)
        return total + jnp.dot(left, rows, preferred_element_type=jnp.float32)

    total = lax.fori_loop(jnp.int32(0), jnp.int32(blocks), one_block, jnp.zeros((PAIRS, NPAIR), jnp.float32))
    ladder = total.astype(jnp.bfloat16).reshape(PAIRS, NAO, NUW)
    forward = jnp.einsum("ma,pmn->pan", coef, ladder.astype(jnp.float32)).astype(jnp.bfloat16)
    return jnp.einsum("pan,nb->pab", forward.astype(jnp.float32), win).astype(jnp.bfloat16)
```

```python
import functools

import jax
import jax.numpy as jnp
from jax import lax
from jax.experimental import pallas as pl
from jax.experimental.pallas import tpu as pltpu
from jax.sharding import Mesh
from jax.sharding import PartitionSpec as P

F32 = jnp.float32
BF16 = jnp.bfloat16
ROWS = (((0,), (0,)), ((), ()))
LANES = (((1,), (1,)), ((), ()))


def iota(shape, dim):
    return lax.broadcasted_iota(jnp.int32, shape, dim)


def div(x, n):
    if n & (n - 1) == 0:
        return lax.shift_right_logical(x, n.bit_length() - 1)
    return lax.shift_right_logical(x * ((1 << 19) // n + 1), 19)


def mod(x, n):
    return x & (n - 1) if n & (n - 1) == 0 else x - div(x, n) * n


def row_ids(size):
    return iota((size, 1), 0)


def lane_ids(size):
    return iota((1, size), 1)


def ones_where(cond):
    return jnp.where(cond, 1.0, 0.0).astype(BF16)


def mm(x, y):
    return jnp.dot(x, y, preferred_element_type=F32)


def half_kernel(
    steps, few, core_ref, amp_hbm, win_hbm, coef_hbm, out_ref, amp_ref, win_ref, coef_ref, sems
):
    total, pairs, _ = amp_hbm.shape
    nuw = win_hbm.shape[0]
    dests, padded, lanes = out_ref.shape
    side, squares, width = 4, 2, 128
    mus = lanes - width
    virt = total // steps
    rows = virt * pairs
    copies = [
        pltpu.make_async_copy(
            amp_hbm.at[step * virt : (step + 1) * virt],
            amp_ref.at[step * virt : (step + 1) * virt],
            sems.at[step],
        )
        for step in range(steps)
    ]
    count = coef_ref.shape[1]
    start = pl.multiple_of(core_ref[0] * count, count)
    win_copy = pltpu.make_async_copy(win_hbm, win_ref, sems.at[steps])
    coef_copy = pltpu.make_async_copy(coef_hbm.at[:, pl.ds(start, count)], coef_ref, sems.at[steps + 1])
    win_copy.start()
    coef_copy.start()
    for copy in copies[:2]:
        copy.start()
    coef_copy.wait()
    coef = coef_ref[...].astype(F32)
    run = mus // (count // (2 * mus))
    blocks = mus // run
    for x in range(side):
        for z in range(squares):
            at = (x * squares + z) * run
            chunk = [coef[:, b * 2 * mus + at : b * 2 * mus + at + run] for b in range(blocks)]
            chunk = jnp.concatenate(chunk, axis=1).astype(BF16)
            for y in range(side):
                dest = (y * squares + z) * side + x
                out_ref[dest, :, :mus] = jnp.zeros((padded, mus), BF16)
                out_ref[dest, :total, :mus] = chunk
    win_copy.wait()
    lane = row_ids(side * width)
    spread = ones_where(div(mod(lane, width), few) == lane_ids(nuw))
    pair_of = div(lane, width) * few + mod(lane, few)
    own = pair_of == mod(lane_ids(rows), pairs)
    gathered = None
    for step in range(steps):
        copies[step].wait()
        if step + 2 < steps:
            copies[step + 2].start()
        block = amp_ref[step * virt : (step + 1) * virt].reshape(rows, amp_ref.shape[2])
        half = lax.dot_general(win_ref[...], block, LANES, preferred_element_type=F32)
        wide = jnp.where(own, mm(spread, half.astype(BF16)), 0.0).astype(BF16)
        collect = ones_where(div(lane_ids(rows), pairs) + step * virt == row_ids(padded))
        part = lax.dot_general(collect, wide, LANES, preferred_element_type=F32)
        gathered = part if gathered is None else gathered + part
    gathered = gathered.astype(BF16)
    for y in range(side):
        for low in range(dests // side):
            out_ref[y * (dests // side) + low, :, mus:] = gathered[:, y * width : (y + 1) * width]


def amp_kernel(nuw, core_ref, in_ref, coef_ref, out_ref):
    parts, padded, lanes = in_ref.shape
    dests, few, cols = out_ref.shape
    width = 128
    mus = lanes - width
    half = in_ref[:, :, mus:].reshape(parts * padded, width)
    every = mus * nuw
    repeat = dests * cols // (2 * every)
    blocks = dests // (2 * repeat)
    rows_of = ones_where(div(row_ids(every), nuw) == lane_ids(mus))
    own = mod(row_ids(every), nuw) == div(lane_ids(width), few)
    pick = ones_where(row_ids(2 * few) == mod(lane_ids(width), few))
    for other in range(2):
        coef = coef_ref[...] if other else in_ref[:, :, :mus]
        coef = coef.reshape(parts * padded, mus)
        amp = lax.dot_general(coef, half, ROWS, preferred_element_type=F32).astype(BF16)
        wide = jnp.where(own, mm(rows_of, amp), 0.0).astype(BF16)
        ordered = lax.dot_general(pick, wide, LANES, preferred_element_type=F32)[:few].astype(BF16)
        for b in range(blocks):
            for zh in range(repeat):
                dest = ((core_ref[0] ^ other) * blocks + b) * repeat + zh
                out_ref[dest] = ordered[:, b * cols : (b + 1) * cols]


def terms_kernel(blk, mask_ref, core_ref, amp_ref, other_amp_ref, ints_ref, out_ref, all_ref):
    step = pl.program_id(0)
    rows, cols = ints_ref.shape
    dests, some, lanes = out_ref.shape
    side, slab = 4, 8
    owners = some // slab
    half = side * some // 2
    some_rows = half // side
    part_cols = amp_ref.shape[1]

    @pl.when(step == 0)
    def _():
        for core, ref in [(core_ref[0], amp_ref), (core_ref[0] ^ 1, other_amp_ref)]:
            for y in range(side):
                at = pl.multiple_of(core * half + y * some_rows, some_rows)
                for z in range(rows // part_cols):
                    start = (y * (rows // part_cols) + z) * some_rows
                    all_ref[pl.ds(at, some_rows), z * part_cols : (z + 1) * part_cols] = ref[
                        start : start + some_rows, :
                    ]

    terms = []
    for col in range(cols // blk):
        total = None
        for row in range(rows // blk):
            keep = mask_ref[row, step * (cols // blk) + col].astype(F32)
            term = keep * mm(
                all_ref[:, row * blk : (row + 1) * blk],
                ints_ref[row * blk : (row + 1) * blk, col * blk : (col + 1) * blk],
            )
            total = term if total is None else total + term
        terms.append(total)
    terms = jnp.concatenate(terms, axis=1)
    for dest in range(dests):
        z, y = dest // side, dest % side
        cut = slice(z * lanes, (z + 1) * lanes)
        part = []
        for o in range(owners):
            at = o % 2 * half + y * some_rows + o // 2 * slab
            part.append(terms[at : at + slab, cut])
        out_ref[dest] = jnp.concatenate(part, axis=0).astype(BF16)


def sum_terms_kernel(nuw, owners, in_ref, out_ref):
    parts, rows, cols = in_ref.shape
    dests, lams, lanes = out_ref.shape
    some = rows // owners
    total = in_ref[0].astype(F32)
    for part in range(1, parts):
        total = total + in_ref[part].astype(F32)
    total = total.astype(BF16)
    wide_rows = owners * lanes
    row = row_ids(wide_rows)
    source = jnp.where(mod(row, lanes) < nuw * some, div(row, lanes) * some + mod(row, some), -1)
    wide = mm(ones_where(source == lane_ids(rows)), total)
    own = div(mod(row, lanes), some) == mod(lane_ids(cols), nuw)
    wide = jnp.where(own, wide, 0.0).astype(BF16)
    collect = ones_where(div(lane_ids(cols), nuw) == row_ids(lams))
    ordered = lax.dot_general(collect, wide, LANES, preferred_element_type=F32).astype(BF16)
    for dest in range(dests):
        o = dest // (dests // owners)
        out_ref[dest] = ordered[:, o * lanes : (o + 1) * lanes]


def forward_kernel(core_ref, in_ref, coef_ref, lad_ref, out_ref):
    dests, padded, lanes = out_ref.shape
    owners, lams, _ = lad_ref.shape
    mus = owners * lams // 2
    fwd = None
    for other in range(2):
        coef = coef_ref[...] if other else in_ref[:, :, :mus]
        start = (core_ref[0] ^ other) * (owners // 2)
        ladder = lad_ref[pl.ds(start, owners // 2)].reshape(mus, lanes)
        part = mm(coef.reshape(dests * padded, mus), ladder)
        fwd = part if fwd is None else fwd + part
    out_ref[...] = fwd.astype(BF16).reshape(out_ref.shape)


def out_kernel(few, fwd_ref, win_ref, out_ref, rows_ref):
    step = pl.program_id(0)
    parts, total, lanes = fwd_ref.shape
    nuw = win_ref.shape[0]
    virt, pairs, _ = out_ref.shape
    side = pairs // few
    rows = virt * pairs

    @pl.when(step == 0)
    def _():
        joined = []
        for y in range(side):
            fwd = None
            for low in range(parts // side):
                part = fwd_ref[y * (parts // side) + low].astype(F32)
                fwd = part if fwd is None else fwd + part
            joined.append(fwd)
        joined = jnp.concatenate(joined, axis=1).astype(BF16)
        every = rows_ref.shape[0]
        spread = ones_where(div(lane_ids(every), pairs) == row_ids(total))
        lane = row_ids(side * lanes)
        pair_of = div(lane, lanes) * few + mod(lane, few)
        pair_of = jnp.where(mod(lane, lanes) < nuw * few, pair_of, -1)
        wide = lax.dot_general(joined, spread, ROWS, preferred_element_type=F32)
        wide = jnp.where(pair_of == mod(lane_ids(every), pairs), wide, 0.0).astype(BF16)
        pick = ones_where(div(mod(lane_ids(side * lanes), lanes), few) == row_ids(rows_ref.shape[1]))
        rows_ref[...] = mm(pick, wide).T.astype(BF16)

    fwd = rows_ref[pl.ds(pl.multiple_of(step * rows, rows), rows), :]
    out_ref[...] = mm(fwd[:, :nuw], win_ref[...]).astype(BF16).reshape(out_ref.shape)


def params(mib=24):
    return pltpu.CompilerParams(vmem_limit_bytes=mib * 1024 * 1024)


def swap(array, axis):
    return lax.ppermute(array, axis, [(0, 1), (1, 0)])


def exchange(array, axes):
    return lax.all_to_all(array, axes, split_axis=0, concat_axis=0, tiled=True)


def local(sizes, amplitudes, window_coef, virtual_coef, integrals, block_mask):
    pairs, virt, _ = amplitudes.shape
    nuw, nv = window_coef.shape
    nao = virtual_coef.shape[0]
    rows, cols = integrals.shape
    side = sizes["y"]
    sp = side * sizes["z"] * sizes["x"]
    op = sizes["zh"] * sizes["core"]
    few = pairs // side
    mus = nao * side // sp
    width = 128
    steps = 4
    padded = -(-virt // 16) * 16
    amp = jnp.transpose(amplitudes, (1, 0, 2))
    coef = jnp.transpose(virtual_coef, (1, 0))
    my_core = lax.axis_index("core").reshape(1)
    smem = pl.BlockSpec(memory_space=pltpu.SMEM)
    hbm = pl.BlockSpec(memory_space=pltpu.HBM)
    vmem = pl.BlockSpec(memory_space=pltpu.VMEM)

    sent = pl.pallas_call(
        functools.partial(half_kernel, steps, few),
        in_specs=[smem, hbm, hbm, hbm],
        out_specs=vmem,
        out_shape=jax.ShapeDtypeStruct((sp, padded, mus // 2 + width), BF16),
        scratch_shapes=[
            pltpu.VMEM((virt, pairs, nv), BF16),
            pltpu.VMEM((nuw, nv), BF16),
            pltpu.VMEM((virt, nao // 2), BF16),
            pltpu.SemaphoreType.DMA((steps + 2,)),
        ],
        compiler_params=params(52),
        name="half",
    )(my_core, amp, window_coef, coef)
    chunk = exchange(sent, ("y", "z", "x"))
    other_coef = swap(chunk[:, :, : mus // 2], "core")
    some = nuw * mus * side // sp
    ao_amp = pl.pallas_call(
        functools.partial(amp_kernel, nuw),
        in_specs=[smem, vmem, vmem],
        out_specs=vmem,
        out_shape=jax.ShapeDtypeStruct((sp // sizes["x"] * sizes["zh"], few, some), BF16),
        compiler_params=params(),
        name="amp",
    )(my_core, chunk, other_coef)
    amp_here = exchange(ao_amp, ("y", "z", "zh")).reshape(-1, some)
    amp_there = swap(amp_here, "core")

    wide = cols // sizes["x"]
    part = wide // sizes["z"]
    whole = lambda array: pl.BlockSpec(array.shape, lambda i: (0, 0))
    terms = pl.pallas_call(
        functools.partial(terms_kernel, rows // block_mask.shape[0]),
        grid=(sizes["x"],),
        in_specs=[
            smem,
            smem,
            whole(amp_here),
            whole(amp_there),
            pl.BlockSpec((rows, wide), lambda i: (0, i)),
        ],
        out_specs=pl.BlockSpec((side * sizes["z"], op * few, part), lambda i: (i, 0, 0)),
        out_shape=jax.ShapeDtypeStruct((sp, op * few, part), BF16),
        scratch_shapes=[pltpu.VMEM((op * pairs, rows), BF16)],
        compiler_params=params(52),
        name="terms",
    )(block_mask, my_core, amp_here, amp_there, integrals)
    pieces = exchange(terms, ("x", "z", "y"))
    ladder = pl.pallas_call(
        functools.partial(sum_terms_kernel, nuw, op),
        out_shape=jax.ShapeDtypeStruct((op, part // nuw, width), BF16),
        compiler_params=params(),
        name="sum_terms",
    )(pieces)
    owned = exchange(ladder, ("zh", "core"))
    fwd = pl.pallas_call(
        forward_kernel,
        in_specs=[smem, vmem, vmem, vmem],
        out_specs=vmem,
        out_shape=jax.ShapeDtypeStruct((sp, padded, width), BF16),
        compiler_params=params(),
        name="forward",
    )(my_core, chunk, other_coef, owned)
    fwd = exchange(fwd, ("y", "z", "x"))
    out = pl.pallas_call(
        functools.partial(out_kernel, few),
        grid=(steps,),
        in_specs=[pl.BlockSpec(fwd.shape, lambda i: (0, 0, 0)), whole(window_coef)],
        out_specs=pl.BlockSpec((virt // steps, pairs, nv), lambda i: (i, 0, 0)),
        out_shape=jax.ShapeDtypeStruct((virt, pairs, nv), BF16),
        scratch_shapes=[pltpu.VMEM((virt * pairs, 16), BF16)],
        compiler_params=params(),
        name="out",
    )(fwd, window_coef)
    return jnp.transpose(out, (1, 0, 2))


def solution(mesh):
    sizes = {"y": 4, "z": 2, "x": 4, "zh": 4, "core": 2}
    fine = Mesh(mesh.devices.reshape(tuple(sizes.values())), tuple(sizes))
    sp, op = ("y", "z", "x"), ("zh", "core")
    placed = (P(op, sp, None), P(), P(None, sp), P(sp, op), P(sp, op))
    return jax.shard_map(
        functools.partial(local, sizes),
        mesh=fine,
        in_specs=placed,
        out_specs=P(op, sp, None),
        check_vma=False,
    )
```

```python
import functools

import jax
import jax.numpy as jnp
from jax import lax
from jax.experimental import pallas as pl
from jax.experimental.pallas import tpu as pltpu
from jax.sharding import Mesh
from jax.sharding import PartitionSpec as P

F32 = jnp.float32
BF16 = jnp.bfloat16
ROWS = (((0,), (0,)), ((), ()))
LANES = (((1,), (1,)), ((), ()))


def iota(shape, dim):
    return lax.broadcasted_iota(jnp.int32, shape, dim)


def div(x, n):
    if n & (n - 1) == 0:
        return lax.shift_right_logical(x, n.bit_length() - 1)
    return lax.shift_right_logical(x * ((1 << 19) // n + 1), 19)


def mod(x, n):
    return x & (n - 1) if n & (n - 1) == 0 else x - div(x, n) * n


def row_ids(size):
    return iota((size, 1), 0)


def lane_ids(size):
    return iota((1, size), 1)


def ones_where(cond):
    return jnp.where(cond, 1.0, 0.0).astype(BF16)


def mm(x, y):
    return jnp.dot(x, y, preferred_element_type=F32)


def repeated(win, few, width):
    nuw, nv = win.shape
    win = jnp.broadcast_to(win.astype(F32)[:, None, :], (nuw, few, nv)).reshape(nuw * few, nv)
    return jnp.concatenate([win, jnp.zeros((width - nuw * few, nv), F32)], axis=0).astype(BF16)


def half_kernel(
    steps, few, core_ref, amp_hbm, win_hbm, coef_hbm, out_ref, amp_ref, win_ref, coef_ref, half_ref, sems
):
    total, pairs, _ = amp_hbm.shape
    dests, padded, lanes = out_ref.shape
    blocks, _, mus = coef_ref.shape
    width = lanes - mus
    side = pairs // few
    virt = total // steps
    rows = virt * pairs
    ahead = 3
    copies = [
        pltpu.make_async_copy(
            amp_hbm.at[step * virt : (step + 1) * virt],
            amp_ref.at[step * virt : (step + 1) * virt],
            sems.at[step],
        )
        for step in range(steps)
    ]
    win_copy = pltpu.make_async_copy(win_hbm, win_ref, sems.at[steps])
    coef_copies = []
    for b in range(blocks):
        start = pl.multiple_of((2 * b + core_ref[0]) * mus, mus)
        coef_copies.append(
            pltpu.make_async_copy(coef_hbm.at[:, pl.ds(start, mus)], coef_ref.at[b], sems.at[steps + 1 + b])
        )
    win_copy.start()
    for copy in copies[:ahead]:
        copy.start()
    for copy in coef_copies:
        copy.start()
    win_copy.wait()
    win = repeated(win_ref[...], few, width)
    own = mod(row_ids(few), few) == mod(lane_ids(width), few)
    out_ref[:, total:, :mus] = jnp.zeros((dests, padded - total, mus), BF16)
    for step in range(steps):
        copies[step].wait()
        if step + ahead < steps:
            copies[step + ahead].start()
        block = amp_ref[step * virt : (step + 1) * virt].reshape(rows, amp_ref.shape[2])
        deep = 768
        half = lax.dot_general(block[:, :deep], win[:, :deep], LANES, preferred_element_type=F32)
        half += lax.dot_general(block[:, deep:], win[:, deep:], LANES, preferred_element_type=F32)
        half = half.astype(BF16).astype(F32).reshape(virt, side, few, width)
        for x in range(side):
            part = jnp.sum(jnp.where(own, half[:, x], 0.0), axis=1)
            half_ref[x, step * virt : (step + 1) * virt, :] = part
        if step == 0:
            for b in range(blocks):
                coef_copies[b].wait()
                for x in range(side):
                    out_ref[b * side + x, :total, :mus] = coef_ref[b]
    half_ref[:, total:, :] = jnp.zeros((side, padded - total, width), F32)
    for x in range(side):
        half = half_ref[x].astype(BF16)
        for b in range(blocks):
            out_ref[b * side + x, :, mus:] = half


def amp_of(nuw, few, half, coef):
    depth, mus = coef.shape
    every = mus * nuw
    width = half.shape[1]
    amp = lax.dot_general(coef, half, ROWS, preferred_element_type=F32).astype(BF16)
    wide = mm(ones_where(div(row_ids(every), nuw) == lane_ids(mus)), amp)
    own = mod(row_ids(every), nuw) == div(lane_ids(width), few)
    wide = jnp.where(own, wide, 0.0).astype(BF16)
    pick = ones_where(row_ids(2 * few) == mod(lane_ids(width), few))
    return lax.dot_general(pick, wide, LANES, preferred_element_type=F32)[:few].astype(BF16)


def own_amp_kernel(nuw, in_ref, out_ref):
    parts, padded, lanes = in_ref.shape
    mus = lanes // 2
    coef = in_ref[:, :, :mus].reshape(parts * padded, mus)
    half = in_ref[:, :, mus:].reshape(parts * padded, mus)
    out_ref[...] = amp_of(nuw, out_ref.shape[0], half, coef)


def amp_kernel(nuw, core_ref, in_ref, coef_ref, own_ref, out_ref):
    parts, padded, lanes = in_ref.shape
    dests, few, cols = out_ref.shape
    mus = lanes // 2
    repeat = dests * cols // (2 * mus * nuw)
    blocks = dests // (2 * repeat)
    half = in_ref[:, :, mus:].reshape(parts * padded, mus)
    other_amp = amp_of(nuw, few, half, coef_ref[...].reshape(parts * padded, mus))
    for other, amp in enumerate([own_ref[...], other_amp]):
        for b in range(blocks):
            for zh in range(repeat):
                dest = ((core_ref[0] ^ other) * blocks + b) * repeat + zh
                out_ref[dest] = amp[:, b * cols : (b + 1) * cols]


def terms_kernel(blk, mask_ref, core_ref, amp_ref, other_amp_ref, ints_ref, out_ref, all_ref):
    step = pl.program_id(0)
    rows, cols = ints_ref.shape
    dests, few, _ = out_ref.shape
    half = amp_ref.shape[0]
    side = 4

    @pl.when(step == 0)
    def _():
        at = pl.multiple_of(core_ref[0] * half, half)
        all_ref[pl.ds(at, half), :] = amp_ref[...]
        at = pl.multiple_of((core_ref[0] ^ 1) * half, half)
        all_ref[pl.ds(at, half), :] = other_amp_ref[...]

    for col in range(cols // blk):
        total = None
        for row in range(rows // blk):
            keep = mask_ref[row, step * (cols // blk) + col].astype(F32)
            term = keep * mm(
                all_ref[:, row * blk : (row + 1) * blk],
                ints_ref[row * blk : (row + 1) * blk, col * blk : (col + 1) * blk],
            )
            total = term if total is None else total + term
        for dest in range(dests):
            o, x = dest // side, dest % side
            at = o % 2 * half + x * (half // side) + o // 2 * few
            out_ref[dest, :, col * blk : (col + 1) * blk] = total[at : at + few].astype(BF16)


def sum_terms_kernel(in_ref, out_ref):
    total = in_ref[0].astype(F32)
    for part in range(1, in_ref.shape[0]):
        total = total + in_ref[part].astype(F32)
    out_ref[...] = total.astype(BF16)


def forward_kernel(nuw, core_ref, in_ref, coef_ref, lad_ref, out_ref, order_ref):
    dests, padded, lanes = out_ref.shape
    few, cols = lad_ref.shape
    mus = cols // nuw // 2
    part_cols = 384
    run = part_cols // nuw
    row = row_ids(lanes)
    source = jnp.where(row < nuw * few, mod(row, few), -1)
    wide = mm(ones_where(source == lane_ids(few)), lad_ref[...])
    own = div(row, few) == mod(lane_ids(part_cols), nuw)
    collect = ones_where(div(lane_ids(part_cols), nuw) == row_ids(run))
    for part in range(cols // part_cols):
        some = wide[:, part * part_cols : (part + 1) * part_cols]
        some = jnp.where(own, some, 0.0).astype(BF16)
        some = lax.dot_general(collect, some, LANES, preferred_element_type=F32)
        order_ref[part * run : (part + 1) * run, :] = some.astype(BF16)
    fwd = None
    for other in range(2):
        coef = coef_ref[...] if other else in_ref[:, :, :mus]
        start = pl.multiple_of((core_ref[0] ^ other) * mus, mus)
        part = mm(coef.reshape(dests * padded, mus), order_ref[pl.ds(start, mus), :])
        fwd = part if fwd is None else fwd + part
    out_ref[...] = fwd.astype(BF16).reshape(out_ref.shape)


def out_kernel(steps, few, fwd_ref, win_ref, out_hbm, out_ref, sems):
    parts, _, lanes = fwd_ref.shape
    total, pairs, nv = out_ref.shape
    side = pairs // few
    virt = total // steps
    win = repeated(win_ref[...], few, lanes)
    own = row_ids(few) == mod(lane_ids(lanes), few)
    fwds = []
    for x in range(side):
        fwd = None
        for block in range(parts // side):
            part = fwd_ref[block * side + x].astype(F32)
            fwd = part if fwd is None else fwd + part
        fwds.append(fwd)
    copies = []
    for step in range(steps):
        cut = slice(step * virt, (step + 1) * virt)
        wide = [jnp.broadcast_to(fwd[cut][:, None, :], (virt, few, lanes)) for fwd in fwds]
        wide = jnp.concatenate([jnp.where(own, part, 0.0) for part in wide], axis=1)
        wide = wide.reshape(virt * pairs, lanes).astype(BF16)
        out_ref[cut] = mm(wide, win).astype(BF16).reshape(virt, pairs, nv)
        copies.append(pltpu.make_async_copy(out_ref.at[cut], out_hbm.at[cut], sems.at[step]))
        copies[-1].start()
    for copy in copies:
        copy.wait()


def params(mib=24):
    return pltpu.CompilerParams(vmem_limit_bytes=mib * 1024 * 1024)


def swap(array, axis):
    return lax.ppermute(array, axis, [(0, 1), (1, 0)])


def turn(array, sizes):
    square = sizes["y"] * sizes["z"]
    pairs = [(one, one % square * square + one // square) for one in range(square * square)]
    return lax.ppermute(array, ("y", "z", "zh", "core"), pairs)


def exchange(array, axes):
    return lax.all_to_all(array, axes, split_axis=0, concat_axis=0, tiled=True)


def local(sizes, amplitudes, window_coef, virtual_coef, integrals, block_mask):
    pairs, virt, _ = amplitudes.shape
    nuw, nv = window_coef.shape
    nao = virtual_coef.shape[0]
    rows, cols = integrals.shape
    side = sizes["y"]
    sp = side * sizes["z"] * sizes["x"]
    op = sizes["zh"] * sizes["core"]
    few = pairs // side
    mus = nao * side // sp
    width = 128
    steps = 4
    padded = -(-virt // 16) * 16
    amp = jnp.transpose(amplitudes, (1, 0, 2))
    coef = jnp.transpose(virtual_coef, (1, 0))
    my_core = lax.axis_index("core").reshape(1)
    smem = pl.BlockSpec(memory_space=pltpu.SMEM)
    hbm = pl.BlockSpec(memory_space=pltpu.HBM)
    vmem = pl.BlockSpec(memory_space=pltpu.VMEM)

    sent = pl.pallas_call(
        functools.partial(half_kernel, steps, few),
        in_specs=[smem, hbm, hbm, hbm],
        out_specs=vmem,
        out_shape=jax.ShapeDtypeStruct((sp, padded, mus // 2 + width), BF16),
        scratch_shapes=[
            pltpu.VMEM((virt, pairs, nv), BF16),
            pltpu.VMEM((nuw, nv), BF16),
            pltpu.VMEM((nao // mus, virt, mus // 2), BF16),
            pltpu.VMEM((side, padded, width), F32),
            pltpu.SemaphoreType.DMA((steps + 1 + nao // mus,)),
        ],
        compiler_params=params(54),
        name="half",
    )(my_core, amp, window_coef, coef)
    chunk = exchange(sent, ("y", "z", "x"))
    other_coef = swap(chunk[:, :, : mus // 2], "core")
    flat = sizes["x"] * sizes["zh"]
    own_amp = pl.pallas_call(
        functools.partial(own_amp_kernel, nuw),
        out_shape=jax.ShapeDtypeStruct((few, mus // 2 * nuw), BF16),
        compiler_params=params(),
        name="own_amp",
    )(chunk)
    ao_amp = pl.pallas_call(
        functools.partial(amp_kernel, nuw),
        in_specs=[smem, vmem, vmem, vmem],
        out_specs=vmem,
        out_shape=jax.ShapeDtypeStruct((flat, few, rows), BF16),
        compiler_params=params(),
        name="amp",
    )(my_core, chunk, other_coef, own_amp)
    amp_here = exchange(ao_amp, ("x", "zh")).reshape(flat * few, rows)
    amp_there = swap(amp_here, "core")

    wide = cols // 4
    whole = lambda array: pl.BlockSpec(array.shape, lambda i: (0, 0))
    terms = pl.pallas_call(
        functools.partial(terms_kernel, rows // block_mask.shape[0]),
        grid=(cols // wide,),
        in_specs=[
            smem,
            smem,
            whole(amp_here),
            whole(amp_there),
            pl.BlockSpec((rows, wide), lambda i: (0, i)),
        ],
        out_specs=pl.BlockSpec((sp, few, wide), lambda i: (0, 0, i)),
        out_shape=jax.ShapeDtypeStruct((sp, few, cols), BF16),
        scratch_shapes=[pltpu.VMEM((op * pairs, rows), BF16)],
        compiler_params=params(24),
        name="terms",
    )(block_mask, my_core, amp_here, amp_there, integrals)
    pieces = exchange(terms, ("y", "z", "x"))
    ladder = pl.pallas_call(
        sum_terms_kernel,
        out_shape=jax.ShapeDtypeStruct((few, cols), BF16),
        compiler_params=params(),
        name="sum_terms",
    )(pieces)
    owned = turn(ladder, sizes)
    fwd = pl.pallas_call(
        functools.partial(forward_kernel, nuw),
        in_specs=[smem, vmem, vmem, vmem],
        out_specs=vmem,
        out_shape=jax.ShapeDtypeStruct((sp, padded, width), BF16),
        scratch_shapes=[pltpu.VMEM((mus, width), BF16)],
        compiler_params=params(),
        name="forward",
    )(my_core, chunk, other_coef, owned)
    fwd = exchange(fwd, ("y", "z", "x"))
    out = pl.pallas_call(
        functools.partial(out_kernel, steps, few),
        in_specs=[vmem, vmem],
        out_specs=hbm,
        out_shape=jax.ShapeDtypeStruct((virt, pairs, nv), BF16),
        scratch_shapes=[pltpu.VMEM((virt, pairs, nv), BF16), pltpu.SemaphoreType.DMA((steps,))],
        compiler_params=params(),
        name="out",
    )(fwd, window_coef)
    return jnp.transpose(out, (1, 0, 2))


def solution(mesh):
    sizes = {"y": 4, "z": 2, "x": 4, "zh": 4, "core": 2}
    fine = Mesh(mesh.devices.reshape(tuple(sizes.values())), tuple(sizes))
    sp, op = ("y", "z", "x"), ("zh", "core")
    placed = (P(op, sp, None), P(), P(None, sp), P(sp, op), P(sp, op))
    return jax.shard_map(
        functools.partial(local, sizes),
        mesh=fine,
        in_specs=placed,
        out_specs=P(op, sp, None),
        check_vma=False,
    )
```

```python
import functools

import jax
import jax.numpy as jnp
from jax import lax
from jax.experimental import pallas as pl
from jax.experimental.pallas import tpu as pltpu
from jax.sharding import Mesh
from jax.sharding import PartitionSpec as P

F32 = jnp.float32
BF16 = jnp.bfloat16
ROWS = (((0,), (0,)), ((), ()))
LANES = (((1,), (1,)), ((), ()))


def iota(shape, dim):
    return lax.broadcasted_iota(jnp.int32, shape, dim)


def div(x, n):
    if n & (n - 1) == 0:
        return lax.shift_right_logical(x, n.bit_length() - 1)
    return lax.shift_right_logical(x * ((1 << 19) // n + 1), 19)


def mod(x, n):
    return x & (n - 1) if n & (n - 1) == 0 else x - div(x, n) * n


def row_ids(size):
    return iota((size, 1), 0)


def lane_ids(size):
    return iota((1, size), 1)


def ones_where(cond):
    return jnp.where(cond, 1.0, 0.0).astype(BF16)


def mm(x, y):
    return jnp.dot(x, y, preferred_element_type=F32)


def repeated(win, few, width):
    nuw, nv = win.shape
    win = jnp.broadcast_to(win.astype(F32)[:, None, :], (nuw, few, nv)).reshape(nuw * few, nv)
    return jnp.concatenate([win, jnp.zeros((width - nuw * few, nv), F32)], axis=0).astype(BF16)


def half_kernel(
    steps, few, core_ref, amp_hbm, win_hbm, coef_hbm, out_ref, amp_ref, win_ref, coef_ref, half_ref, sems
):
    total, pairs, _ = amp_hbm.shape
    dests, padded, lanes = out_ref.shape
    blocks, _, mus = coef_ref.shape
    width = lanes - mus
    side = pairs // few
    virt = total // steps
    rows = virt * pairs
    ahead = 5
    copies = [
        pltpu.make_async_copy(
            amp_hbm.at[step * virt : (step + 1) * virt],
            amp_ref.at[step * virt : (step + 1) * virt],
            sems.at[step],
        )
        for step in range(steps)
    ]
    win_copy = pltpu.make_async_copy(win_hbm, win_ref, sems.at[steps])
    coef_copies = []
    for b in range(blocks):
        start = pl.multiple_of((2 * b + core_ref[0]) * mus, mus)
        coef_copies.append(
            pltpu.make_async_copy(coef_hbm.at[:, pl.ds(start, mus)], coef_ref.at[b], sems.at[steps + 1 + b])
        )
    win_copy.start()
    for copy in copies[:ahead]:
        copy.start()
    for copy in coef_copies:
        copy.start()
    win_copy.wait()
    spread = ones_where(div(lane_ids(width), few) == row_ids(win_ref.shape[0]))
    win = lax.dot_general(win_ref[...], spread, ROWS, preferred_element_type=F32).astype(BF16)
    own = mod(row_ids(few), few) == mod(lane_ids(width), few)
    out_ref[:, total:, :mus] = jnp.zeros((dests, padded - total, mus), BF16)
    for step in range(steps):
        copies[step].wait()
        if step + ahead < steps:
            copies[step + ahead].start()
        block = amp_ref[step * virt : (step + 1) * virt].reshape(rows, amp_ref.shape[2])
        half = mm(block, win)
        half = half.astype(BF16).astype(F32).reshape(virt, side, few, width)
        for x in range(side):
            part = jnp.sum(jnp.where(own, half[:, x], 0.0), axis=1)
            half_ref[x, step * virt : (step + 1) * virt, :] = part
        if step == 0:
            for b in range(blocks):
                coef_copies[b].wait()
                for x in range(side):
                    out_ref[b * side + x, :total, :mus] = coef_ref[b]
    half_ref[:, total:, :] = jnp.zeros((side, padded - total, width), F32)
    for x in range(side):
        half = half_ref[x].astype(BF16)
        for b in range(blocks):
            out_ref[b * side + x, :, mus:] = half


def amp_of(nuw, few, half, coef):
    depth, mus = coef.shape
    every = mus * nuw
    width = half.shape[1]
    amp = lax.dot_general(coef, half, ROWS, preferred_element_type=F32).astype(BF16)
    wide = mm(ones_where(div(row_ids(every), nuw) == lane_ids(mus)), amp)
    own = mod(row_ids(every), nuw) == div(lane_ids(width), few)
    wide = jnp.where(own, wide, 0.0).astype(BF16)
    pick = ones_where(row_ids(2 * few) == mod(lane_ids(width), few))
    return lax.dot_general(pick, wide, LANES, preferred_element_type=F32)[:few].astype(BF16)


def own_amp_kernel(nuw, in_ref, out_ref):
    parts, padded, lanes = in_ref.shape
    mus = lanes // 2
    coef = in_ref[:, :, :mus].reshape(parts * padded, mus)
    half = in_ref[:, :, mus:].reshape(parts * padded, mus)
    out_ref[...] = amp_of(nuw, out_ref.shape[0], half, coef)


def amp_kernel(nuw, core_ref, in_ref, coef_ref, own_ref, out_ref):
    parts, padded, lanes = in_ref.shape
    dests, few, cols = out_ref.shape
    mus = lanes // 2
    repeat = dests * cols // (2 * mus * nuw)
    blocks = dests // (2 * repeat)
    half = in_ref[:, :, mus:].reshape(parts * padded, mus)
    other_amp = amp_of(nuw, few, half, coef_ref[...].reshape(parts * padded, mus))
    for other, amp in enumerate([own_ref[...], other_amp]):
        for b in range(blocks):
            for zh in range(repeat):
                dest = ((core_ref[0] ^ other) * blocks + b) * repeat + zh
                out_ref[dest] = amp[:, b * cols : (b + 1) * cols]


def terms_kernel(blk, mask_ref, core_ref, amp_ref, other_amp_ref, ints_ref, out_ref, all_ref):
    step = pl.program_id(0)
    rows, cols = ints_ref.shape
    dests, few, _ = out_ref.shape
    half = amp_ref.shape[0]
    side = 4

    @pl.when(step == 0)
    def _():
        at = pl.multiple_of(core_ref[0] * half, half)
        all_ref[pl.ds(at, half), :] = amp_ref[...]
        at = pl.multiple_of((core_ref[0] ^ 1) * half, half)
        all_ref[pl.ds(at, half), :] = other_amp_ref[...]

    for col in range(cols // blk):
        kept = []
        for row in range(rows // blk):
            keep = mask_ref[row, step * (cols // blk) + col].astype(F32).astype(BF16)
            kept.append(all_ref[:, row * blk : (row + 1) * blk] * keep)
        kept = jnp.concatenate(kept, axis=1)
        total = mm(kept, ints_ref[:, col * blk : (col + 1) * blk])
        for dest in range(dests):
            o, x = dest // side, dest % side
            at = o % 2 * half + x * (half // side) + o // 2 * few
            out_ref[dest, :, col * blk : (col + 1) * blk] = total[at : at + few].astype(BF16)


def sum_terms_kernel(in_ref, out_ref):
    total = in_ref[0].astype(F32)
    for part in range(1, in_ref.shape[0]):
        total = total + in_ref[part].astype(F32)
    out_ref[...] = total.astype(BF16)


def forward_kernel(nuw, core_ref, in_ref, coef_ref, lad_ref, out_ref, order_ref):
    dests, padded, lanes = out_ref.shape
    few, cols = lad_ref.shape
    mus = cols // nuw // 2
    part_cols = 384
    run = part_cols // nuw
    row = row_ids(lanes)
    source = jnp.where(row < nuw * few, mod(row, few), -1)
    wide = mm(ones_where(source == lane_ids(few)), lad_ref[...])
    own = div(row, few) == mod(lane_ids(part_cols), nuw)
    collect = ones_where(div(lane_ids(part_cols), nuw) == row_ids(run))
    for part in range(cols // part_cols):
        some = wide[:, part * part_cols : (part + 1) * part_cols]
        some = jnp.where(own, some, 0.0).astype(BF16)
        some = lax.dot_general(collect, some, LANES, preferred_element_type=F32)
        order_ref[part * run : (part + 1) * run, :] = some.astype(BF16)
    fwd = None
    for other in range(2):
        coef = coef_ref[...] if other else in_ref[:, :, :mus]
        start = pl.multiple_of((core_ref[0] ^ other) * mus, mus)
        part = mm(coef.reshape(dests * padded, mus), order_ref[pl.ds(start, mus), :])
        fwd = part if fwd is None else fwd + part
    out_ref[...] = fwd.astype(BF16).reshape(out_ref.shape)


def out_kernel(steps, few, fwd_ref, win_ref, out_hbm, out_ref, sems):
    parts, _, lanes = fwd_ref.shape
    total, pairs, nv = out_ref.shape
    side = pairs // few
    virt = total // steps
    win = repeated(win_ref[...], few, lanes)
    own = row_ids(few) == mod(lane_ids(lanes), few)
    fwds = []
    for x in range(side):
        fwd = None
        for block in range(parts // side):
            part = fwd_ref[block * side + x].astype(F32)
            fwd = part if fwd is None else fwd + part
        fwds.append(fwd)
    copies = []
    for step in range(steps):
        cut = slice(step * virt, (step + 1) * virt)
        wide = [jnp.broadcast_to(fwd[cut][:, None, :], (virt, few, lanes)) for fwd in fwds]
        wide = jnp.concatenate([jnp.where(own, part, 0.0) for part in wide], axis=1)
        wide = wide.reshape(virt * pairs, lanes).astype(BF16)
        out_ref[cut] = mm(wide, win).astype(BF16).reshape(virt, pairs, nv)
        copies.append(pltpu.make_async_copy(out_ref.at[cut], out_hbm.at[cut], sems.at[step]))
        copies[-1].start()
    for copy in copies:
        copy.wait()


def params(mib=24):
    return pltpu.CompilerParams(vmem_limit_bytes=mib * 1024 * 1024)


def swap(array, axis):
    return lax.ppermute(array, axis, [(0, 1), (1, 0)])


def turn(array, sizes):
    square = sizes["y"] * sizes["z"]
    pairs = [(one, one % square * square + one // square) for one in range(square * square)]
    return lax.ppermute(array, ("y", "z", "zh", "core"), pairs)


def exchange(array, axes):
    return lax.all_to_all(array, axes, split_axis=0, concat_axis=0, tiled=True)


def local(sizes, amplitudes, window_coef, virtual_coef, integrals, block_mask):
    pairs, virt, _ = amplitudes.shape
    nuw, nv = window_coef.shape
    nao = virtual_coef.shape[0]
    rows, cols = integrals.shape
    side = sizes["y"]
    sp = side * sizes["z"] * sizes["x"]
    op = sizes["zh"] * sizes["core"]
    few = pairs // side
    mus = nao * side // sp
    width = 128
    steps, chunks = 4, 11
    padded = -(-virt // 16) * 16
    amp = jnp.transpose(amplitudes, (1, 0, 2))
    coef = jnp.transpose(virtual_coef, (1, 0))
    my_core = lax.axis_index("core").reshape(1)
    smem = pl.BlockSpec(memory_space=pltpu.SMEM)
    hbm = pl.BlockSpec(memory_space=pltpu.HBM)
    vmem = pl.BlockSpec(memory_space=pltpu.VMEM)

    sent = pl.pallas_call(
        functools.partial(half_kernel, chunks, few),
        in_specs=[smem, hbm, hbm, hbm],
        out_specs=vmem,
        out_shape=jax.ShapeDtypeStruct((sp, padded, mus // 2 + width), BF16),
        scratch_shapes=[
            pltpu.VMEM((virt, pairs, nv), BF16),
            pltpu.VMEM((nuw, nv), BF16),
            pltpu.VMEM((nao // mus, virt, mus // 2), BF16),
            pltpu.VMEM((side, padded, width), F32),
            pltpu.SemaphoreType.DMA((chunks + 1 + nao // mus,)),
        ],
        compiler_params=params(54),
        name="half",
    )(my_core, amp, window_coef, coef)
    chunk = exchange(sent, ("y", "z", "x"))
    other_coef = swap(chunk[:, :, : mus // 2], "core")
    flat = sizes["x"] * sizes["zh"]
    own_amp = pl.pallas_call(
        functools.partial(own_amp_kernel, nuw),
        out_shape=jax.ShapeDtypeStruct((few, mus // 2 * nuw), BF16),
        compiler_params=params(),
        name="own_amp",
    )(chunk)
    ao_amp = pl.pallas_call(
        functools.partial(amp_kernel, nuw),
        in_specs=[smem, vmem, vmem, vmem],
        out_specs=vmem,
        out_shape=jax.ShapeDtypeStruct((flat, few, rows), BF16),
        compiler_params=params(),
        name="amp",
    )(my_core, chunk, other_coef, own_amp)
    amp_here = exchange(ao_amp, ("x", "zh")).reshape(flat * few, rows)
    amp_there = swap(amp_here, "core")

    wide = cols // 4
    whole = lambda array: pl.BlockSpec(array.shape, lambda i: (0, 0))
    terms = pl.pallas_call(
        functools.partial(terms_kernel, rows // block_mask.shape[0]),
        grid=(cols // wide,),
        in_specs=[
            smem,
            smem,
            whole(amp_here),
            whole(amp_there),
            pl.BlockSpec((rows, wide), lambda i: (0, i)),
        ],
        out_specs=pl.BlockSpec((sp, few, wide), lambda i: (0, 0, i)),
        out_shape=jax.ShapeDtypeStruct((sp, few, cols), BF16),
        scratch_shapes=[pltpu.VMEM((op * pairs, rows), BF16)],
        compiler_params=params(24),
        name="terms",
    )(block_mask, my_core, amp_here, amp_there, integrals)
    pieces = exchange(terms, ("y", "z", "x"))
    ladder = pl.pallas_call(
        sum_terms_kernel,
        out_shape=jax.ShapeDtypeStruct((few, cols), BF16),
        compiler_params=params(),
        name="sum_terms",
    )(pieces)
    owned = turn(ladder, sizes)
    fwd = pl.pallas_call(
        functools.partial(forward_kernel, nuw),
        in_specs=[smem, vmem, vmem, vmem],
        out_specs=vmem,
        out_shape=jax.ShapeDtypeStruct((sp, padded, width), BF16),
        scratch_shapes=[pltpu.VMEM((mus, width), BF16)],
        compiler_params=params(),
        name="forward",
    )(my_core, chunk, other_coef, owned)
    fwd = exchange(fwd, ("y", "z", "x"))
    out = pl.pallas_call(
        functools.partial(out_kernel, steps, few),
        in_specs=[vmem, vmem],
        out_specs=hbm,
        out_shape=jax.ShapeDtypeStruct((virt, pairs, nv), BF16),
        scratch_shapes=[pltpu.VMEM((virt, pairs, nv), BF16), pltpu.SemaphoreType.DMA((steps,))],
        compiler_params=params(),
        name="out",
    )(fwd, window_coef)
    return jnp.transpose(out, (1, 0, 2))


def solution(mesh):
    sizes = {"y": 4, "z": 2, "x": 4, "zh": 4, "core": 2}
    fine = Mesh(mesh.devices.reshape(tuple(sizes.values())), tuple(sizes))
    sp, op = ("y", "z", "x"), ("zh", "core")
    placed = (P(op, sp, None), P(), P(None, sp), P(sp, op), P(sp, op))
    return jax.shard_map(
        functools.partial(local, sizes),
        mesh=fine,
        in_specs=placed,
        out_specs=P(op, sp, None),
        check_vma=False,
    )
```

```python
import functools

import jax
import jax.numpy as jnp
from jax import lax
from jax.experimental import pallas as pl
from jax.experimental.pallas import tpu as pltpu
from jax.sharding import Mesh
from jax.sharding import PartitionSpec as P

F32 = jnp.float32
BF16 = jnp.bfloat16
ROWS = (((0,), (0,)), ((), ()))
LANES = (((1,), (1,)), ((), ()))


def iota(shape, dim):
    return lax.broadcasted_iota(jnp.int32, shape, dim)


def div(x, n):
    if n & (n - 1) == 0:
        return lax.shift_right_logical(x, n.bit_length() - 1)
    return lax.shift_right_logical(x * ((1 << 19) // n + 1), 19)


def mod(x, n):
    return x & (n - 1) if n & (n - 1) == 0 else x - div(x, n) * n


def row_ids(size):
    return iota((size, 1), 0)


def lane_ids(size):
    return iota((1, size), 1)


def ones_where(cond):
    return jnp.where(cond, 1.0, 0.0).astype(BF16)


def mm(x, y):
    return jnp.dot(x, y, preferred_element_type=F32)


def repeated(win, few, width):
    nuw, nv = win.shape
    win = jnp.broadcast_to(win.astype(F32)[:, None, :], (nuw, few, nv)).reshape(nuw * few, nv)
    return jnp.concatenate([win, jnp.zeros((width - nuw * few, nv), F32)], axis=0).astype(BF16)


def half_kernel(
    steps, few, core_ref, amp_hbm, win_hbm, coef_hbm, out_ref, amp_ref, win_ref, coef_ref, half_ref, sems
):
    total, pairs, _ = amp_hbm.shape
    dests, packed, lanes = out_ref.shape
    blocks, _, mus = coef_ref.shape
    width = lanes - mus
    side = pairs // few
    virt = total // steps
    rows = virt * pairs
    ahead = 3
    copies = [
        pltpu.make_async_copy(
            amp_hbm.at[step * virt : (step + 1) * virt],
            amp_ref.at[step * virt : (step + 1) * virt],
            sems.at[step],
        )
        for step in range(steps)
    ]
    win_copy = pltpu.make_async_copy(win_hbm, win_ref, sems.at[steps])
    coef_copies = []
    for b in range(blocks):
        start = pl.multiple_of((2 * b + core_ref[0]) * mus, mus)
        coef_copies.append(
            pltpu.make_async_copy(coef_hbm.at[:, pl.ds(start, mus)], coef_ref.at[b], sems.at[steps + 1 + b])
        )
    win_copy.start()
    for copy in copies[:ahead]:
        copy.start()
    for copy in coef_copies:
        copy.start()
    win_copy.wait()
    win = repeated(win_ref[...], few, width)
    own = mod(row_ids(few), few) == mod(lane_ids(width), few)
    for step in range(steps):
        copies[step].wait()
        if step + ahead < steps:
            copies[step + ahead].start()
        block = amp_ref[step * virt : (step + 1) * virt].reshape(rows, amp_ref.shape[2])
        half = lax.dot_general(block, win, LANES, preferred_element_type=F32)
        half = half.astype(BF16).astype(F32).reshape(virt, side, few, width)
        for x in range(side):
            part = jnp.sum(jnp.where(own, half[:, x], 0.0), axis=1)
            half_ref[x, step * virt : (step + 1) * virt, :] = part
    cols = win_hbm.shape[0] * few
    free = width - cols
    for b in range(blocks):
        coef_copies[b].wait()
        coef = coef_ref[b].astype(F32)
        for x in range(side):
            half = half_ref[x]
            rest = [coef[packed:, at : at + free] for at in range(0, mus, free)]
            rest += [half[packed:, at : at + free] for at in range(0, cols, free)]
            rest.append(jnp.zeros((packed - len(rest) * (total - packed), free), F32))
            rest = jnp.concatenate(rest, axis=0)
            half = jnp.concatenate([half[:packed, :cols], rest], axis=1)
            out_ref[b * side + x, :, :mus] = coef[:packed].astype(BF16)
            out_ref[b * side + x, :, mus:] = half.astype(BF16)


def amp_of(nuw, few, half, coef):
    depth, mus = coef.shape
    every = mus * nuw
    width = half.shape[1]
    amp = lax.dot_general(coef, half, ROWS, preferred_element_type=F32).astype(BF16)
    wide = mm(ones_where(div(row_ids(every), nuw) == lane_ids(mus)), amp)
    own = mod(row_ids(every), nuw) == div(lane_ids(width), few)
    wide = jnp.where(own, wide, 0.0).astype(BF16)
    pick = ones_where(row_ids(2 * few) == mod(lane_ids(width), few))
    return lax.dot_general(pick, wide, LANES, preferred_element_type=F32)[:few].astype(BF16)


def unpack_kernel(cols, last, in_ref, coef_ref, half_ref):
    parts, packed, lanes = in_ref.shape
    mus = lanes // 2
    free = mus - cols
    whole = in_ref[...].astype(F32)
    rest = whole[:, :, mus + cols :]
    none = jnp.zeros((parts, coef_ref.shape[1] - packed - last, mus), F32)
    count = mus // free
    coef = [rest[:, i * last : (i + 1) * last] for i in range(count)]
    coef = jnp.concatenate([whole[:, :, :mus], jnp.concatenate(coef, axis=2), none], axis=1)
    coef_ref[...] = coef.astype(BF16)
    half = [rest[:, i * last : (i + 1) * last] for i in range(count, count + cols // free)]
    half.append(jnp.zeros((parts, last, free), F32))
    half = jnp.concatenate([whole[:, :, mus:], jnp.concatenate(half, axis=2), none], axis=1)
    half_ref[...] = half.astype(BF16)


def own_amp_kernel(nuw, half_ref, coef_ref, out_ref):
    parts, padded, mus = coef_ref.shape
    coef = coef_ref[...].reshape(parts * padded, mus)
    half = half_ref[...].reshape(parts * padded, mus)
    out_ref[...] = amp_of(nuw, out_ref.shape[0], half, coef)


def amp_kernel(nuw, core_ref, half_ref, coef_ref, own_ref, out_ref):
    parts, padded, mus = coef_ref.shape
    dests, few, cols = out_ref.shape
    repeat = dests * cols // (2 * mus * nuw)
    blocks = dests // (2 * repeat)
    half = half_ref[...].reshape(parts * padded, mus)
    other_amp = amp_of(nuw, few, half, coef_ref[...].reshape(parts * padded, mus))
    for other, amp in enumerate([own_ref[...], other_amp]):
        for b in range(blocks):
            for zh in range(repeat):
                dest = ((core_ref[0] ^ other) * blocks + b) * repeat + zh
                out_ref[dest] = amp[:, b * cols : (b + 1) * cols]


def terms_kernel(blk, mask_ref, core_ref, amp_ref, other_amp_ref, ints_ref, out_ref, all_ref):
    rows, cols = ints_ref.shape
    dests, few, _ = out_ref.shape
    half = amp_ref.shape[0]
    side = 4
    at = pl.multiple_of(core_ref[0] * half, half)
    all_ref[pl.ds(at, half), :] = amp_ref[...]
    at = pl.multiple_of((core_ref[0] ^ 1) * half, half)
    all_ref[pl.ds(at, half), :] = other_amp_ref[...]
    for col in range(cols // blk):
        total = None
        for row in range(rows // blk):
            keep = mask_ref[row, col].astype(F32)
            term = keep * mm(
                all_ref[:, row * blk : (row + 1) * blk],
                ints_ref[row * blk : (row + 1) * blk, col * blk : (col + 1) * blk],
            )
            total = term if total is None else total + term
        for dest in range(dests):
            o, x = dest // side, dest % side
            at = o % 2 * half + x * (half // side) + o // 2 * few
            out_ref[dest, :, col * blk : (col + 1) * blk] = total[at : at + few].astype(BF16)


def sum_terms_kernel(in_ref, out_ref):
    total = in_ref[0].astype(F32)
    for part in range(1, in_ref.shape[0]):
        total = total + in_ref[part].astype(F32)
    out_ref[...] = total.astype(BF16)


def forward_kernel(nuw, last, core_ref, coef_ref, other_coef_ref, lad_ref, out_ref, order_ref):
    dests, packed, lanes = out_ref.shape
    padded = coef_ref.shape[1]
    few, cols = lad_ref.shape
    mus = cols // nuw // 2
    part_cols = 384
    run = part_cols // nuw
    row = row_ids(lanes)
    source = jnp.where(row < nuw * few, mod(row, few), -1)
    wide = mm(ones_where(source == lane_ids(few)), lad_ref[...])
    own = div(row, few) == mod(lane_ids(part_cols), nuw)
    collect = ones_where(div(lane_ids(part_cols), nuw) == row_ids(run))
    for part in range(cols // part_cols):
        some = wide[:, part * part_cols : (part + 1) * part_cols]
        some = jnp.where(own, some, 0.0).astype(BF16)
        some = lax.dot_general(collect, some, LANES, preferred_element_type=F32)
        order_ref[part * run : (part + 1) * run, :] = some.astype(BF16)
    fwd = None
    for other in range(2):
        coef = (other_coef_ref if other else coef_ref)[...]
        start = pl.multiple_of((core_ref[0] ^ other) * mus, mus)
        part = mm(coef.reshape(dests * padded, mus), order_ref[pl.ds(start, mus), :])
        fwd = part if fwd is None else fwd + part
    fwd = fwd.reshape(dests, padded, lanes)
    used = nuw * few
    free = lanes - used
    rest = [fwd[:, packed : packed + last, at : at + free] for at in range(0, used, free)]
    rest.append(jnp.zeros((dests, packed - len(rest) * last, free), F32))
    fwd = jnp.concatenate([fwd[:, :packed, :used], jnp.concatenate(rest, axis=1)], axis=2)
    out_ref[...] = fwd.astype(BF16)


def out_kernel(steps, few, fwd_ref, win_ref, out_hbm, out_ref, sems):
    parts, packed, lanes = fwd_ref.shape
    total, pairs, nv = out_ref.shape
    last = total - packed
    used = win_ref.shape[0] * few
    free = lanes - used
    side = pairs // few
    virt = total // steps
    win = repeated(win_ref[...], few, lanes)
    own = row_ids(few) == mod(lane_ids(lanes), few)
    fwds = []
    for x in range(side):
        fwd = None
        for block in range(parts // side):
            part = fwd_ref[block * side + x].astype(F32)
            fwd = part if fwd is None else fwd + part
        rest = [fwd[i * last : (i + 1) * last, used:] for i in range(used // free)]
        rest.append(jnp.zeros((last, free), F32))
        fwds.append(jnp.concatenate([fwd, jnp.concatenate(rest, axis=1)], axis=0))
    copies = []
    for step in range(steps):
        cut = slice(step * virt, (step + 1) * virt)
        wide = [jnp.broadcast_to(fwd[cut][:, None, :], (virt, few, lanes)) for fwd in fwds]
        wide = jnp.concatenate([jnp.where(own, part, 0.0) for part in wide], axis=1)
        wide = wide.reshape(virt * pairs, lanes).astype(BF16)
        out_ref[cut] = mm(wide, win).astype(BF16).reshape(virt, pairs, nv)
        copies.append(pltpu.make_async_copy(out_ref.at[cut], out_hbm.at[cut], sems.at[step]))
        copies[-1].start()
    for copy in copies:
        copy.wait()


def params(mib=24):
    return pltpu.CompilerParams(vmem_limit_bytes=mib * 1024 * 1024)


def swap(array, axis):
    return lax.ppermute(array, axis, [(0, 1), (1, 0)])


def turn(array, sizes):
    square = sizes["y"] * sizes["z"]
    pairs = [(one, one % square * square + one // square) for one in range(square * square)]
    return lax.ppermute(array, ("y", "z", "zh", "core"), pairs)


def exchange(array, axes):
    return lax.all_to_all(array, axes, split_axis=0, concat_axis=0, tiled=True)


def local(sizes, amplitudes, window_coef, virtual_coef, integrals, block_mask):
    pairs, virt, _ = amplitudes.shape
    nuw, nv = window_coef.shape
    nao = virtual_coef.shape[0]
    rows, cols = integrals.shape
    side = sizes["y"]
    sp = side * sizes["z"] * sizes["x"]
    op = sizes["zh"] * sizes["core"]
    few = pairs // side
    mus = nao * side // sp
    width = 128
    steps = 4
    padded, packed = -(-virt // 16) * 16, virt // 8 * 8
    amp = jnp.transpose(amplitudes, (1, 0, 2))
    coef = jnp.transpose(virtual_coef, (1, 0))
    my_core = lax.axis_index("core").reshape(1)
    smem = pl.BlockSpec(memory_space=pltpu.SMEM)
    hbm = pl.BlockSpec(memory_space=pltpu.HBM)
    vmem = pl.BlockSpec(memory_space=pltpu.VMEM)

    sent = pl.pallas_call(
        functools.partial(half_kernel, steps, few),
        in_specs=[smem, hbm, hbm, hbm],
        out_specs=vmem,
        out_shape=jax.ShapeDtypeStruct((sp, packed, mus // 2 + width), BF16),
        scratch_shapes=[
            pltpu.VMEM((virt, pairs, nv), BF16),
            pltpu.VMEM((nuw, nv), BF16),
            pltpu.VMEM((nao // mus, virt, mus // 2), BF16),
            pltpu.VMEM((side, virt, width), F32),
            pltpu.SemaphoreType.DMA((steps + 1 + nao // mus,)),
        ],
        compiler_params=params(54),
        name="half",
    )(my_core, amp, window_coef, coef)
    chunk = exchange(sent, ("y", "z", "x"))
    own_coef, half = pl.pallas_call(
        functools.partial(unpack_kernel, nuw * few, virt - packed),
        out_shape=[jax.ShapeDtypeStruct((sp, padded, width), BF16)] * 2,
        compiler_params=params(),
        name="unpack",
    )(chunk)
    other_coef = swap(own_coef, "core")
    flat = sizes["x"] * sizes["zh"]
    own_amp = pl.pallas_call(
        functools.partial(own_amp_kernel, nuw),
        out_shape=jax.ShapeDtypeStruct((few, mus // 2 * nuw), BF16),
        compiler_params=params(),
        name="own_amp",
    )(half, own_coef)
    ao_amp = pl.pallas_call(
        functools.partial(amp_kernel, nuw),
        in_specs=[smem, vmem, vmem, vmem],
        out_specs=vmem,
        out_shape=jax.ShapeDtypeStruct((flat, few, rows), BF16),
        compiler_params=params(),
        name="amp",
    )(my_core, half, other_coef, own_amp)
    amp_here = exchange(ao_amp, ("x", "zh")).reshape(flat * few, rows)
    amp_there = swap(amp_here, "core")

    terms = pl.pallas_call(
        functools.partial(terms_kernel, rows // block_mask.shape[0]),
        in_specs=[smem, smem, vmem, vmem, vmem],
        out_specs=vmem,
        out_shape=jax.ShapeDtypeStruct((sp, few, cols), BF16),
        scratch_shapes=[pltpu.VMEM((op * pairs, rows), BF16)],
        compiler_params=params(),
        name="terms",
    )(block_mask, my_core, amp_here, amp_there, integrals)
    pieces = exchange(terms, ("y", "z", "x"))
    ladder = pl.pallas_call(
        sum_terms_kernel,
        out_shape=jax.ShapeDtypeStruct((few, cols), BF16),
        compiler_params=params(),
        name="sum_terms",
    )(pieces)
    owned = turn(ladder, sizes)
    fwd = pl.pallas_call(
        functools.partial(forward_kernel, nuw, virt - packed),
        in_specs=[smem, vmem, vmem, vmem],
        out_specs=vmem,
        out_shape=jax.ShapeDtypeStruct((sp, packed, width), BF16),
        scratch_shapes=[pltpu.VMEM((mus, width), BF16)],
        compiler_params=params(),
        name="forward",
    )(my_core, own_coef, other_coef, owned)
    fwd = exchange(fwd, ("y", "z", "x"))
    out = pl.pallas_call(
        functools.partial(out_kernel, steps, few),
        in_specs=[vmem, vmem],
        out_specs=hbm,
        out_shape=jax.ShapeDtypeStruct((virt, pairs, nv), BF16),
        scratch_shapes=[pltpu.VMEM((virt, pairs, nv), BF16), pltpu.SemaphoreType.DMA((steps,))],
        compiler_params=params(),
        name="out",
    )(fwd, window_coef)
    return jnp.transpose(out, (1, 0, 2))


def solution(mesh):
    sizes = {"y": 4, "z": 2, "x": 4, "zh": 4, "core": 2}
    fine = Mesh(mesh.devices.reshape(tuple(sizes.values())), tuple(sizes))
    sp, op = ("y", "z", "x"), ("zh", "core")
    placed = (P(op, sp, None), P(), P(None, sp), P(sp, op), P(sp, op))
    return jax.shard_map(
        functools.partial(local, sizes),
        mesh=fine,
        in_specs=placed,
        out_specs=P(op, sp, None),
        check_vma=False,
    )
```

```python
import functools

import jax
import jax.numpy as jnp
from jax import lax
from jax.experimental import pallas as pl
from jax.experimental.pallas import tpu as pltpu
from jax.sharding import Mesh
from jax.sharding import PartitionSpec as P

F32 = jnp.float32
BF16 = jnp.bfloat16
ROWS = (((0,), (0,)), ((), ()))
LANES = (((1,), (1,)), ((), ()))


def iota(shape, dim):
    return lax.broadcasted_iota(jnp.int32, shape, dim)


def div(x, n):
    if n & (n - 1) == 0:
        return lax.shift_right_logical(x, n.bit_length() - 1)
    return lax.shift_right_logical(x * ((1 << 19) // n + 1), 19)


def mod(x, n):
    return x & (n - 1) if n & (n - 1) == 0 else x - div(x, n) * n


def row_ids(size):
    return iota((size, 1), 0)


def lane_ids(size):
    return iota((1, size), 1)


def ones_where(cond):
    return jnp.where(cond, 1.0, 0.0).astype(BF16)


def mm(x, y):
    return jnp.dot(x, y, preferred_element_type=F32)


def repeated(win, few, width):
    nuw, nv = win.shape
    win = jnp.broadcast_to(win.astype(F32)[:, None, :], (nuw, few, nv)).reshape(nuw * few, nv)
    return jnp.concatenate([win, jnp.zeros((width - nuw * few, nv), F32)], axis=0).astype(BF16)


def half_kernel(
    steps, few, core_ref, amp_hbm, win_hbm, coef_hbm, out_ref, amp_ref, win_ref, coef_ref, half_ref, rest_ref, sems
):
    total, pairs, _ = amp_hbm.shape
    dests, packed, lanes = out_ref.shape
    blocks, _, mus = coef_ref.shape
    width = lanes - mus
    side = pairs // few
    last = total - packed
    cols = win_hbm.shape[0] * few
    free = width - cols
    virt = total // steps
    rows = virt * pairs
    ahead = 3
    copies = [
        pltpu.make_async_copy(
            amp_hbm.at[step * virt : (step + 1) * virt],
            amp_ref.at[step * virt : (step + 1) * virt],
            sems.at[step],
        )
        for step in range(steps)
    ]
    win_copy = pltpu.make_async_copy(win_hbm, win_ref, sems.at[steps])
    coef_copies = []
    for b in range(blocks):
        start = pl.multiple_of((2 * b + core_ref[0]) * mus, mus)
        coef_copies.append(
            pltpu.make_async_copy(coef_hbm.at[:, pl.ds(start, mus)], coef_ref.at[b], sems.at[steps + 1 + b])
        )
    win_copy.start()
    for copy in copies[:ahead]:
        copy.start()
    for copy in coef_copies:
        copy.start()
    win_copy.wait()
    win = repeated(win_ref[...], few, width)
    own = mod(row_ids(few), few) == mod(lane_ids(width), few)
    for step in range(steps):
        copies[step].wait()
        if step + ahead < steps:
            copies[step + ahead].start()
        block = amp_ref[step * virt : (step + 1) * virt].reshape(rows, amp_ref.shape[2])
        half = lax.dot_general(block, win, LANES, preferred_element_type=F32)
        half = half.astype(BF16).astype(F32).reshape(virt, side, few, width)
        for x in range(side):
            part = jnp.sum(jnp.where(own, half[:, x], 0.0), axis=1)
            half_ref[x, step * virt : (step + 1) * virt, :] = part
        if step == 0:
            for b in range(blocks):
                coef_copies[b].wait()
                coef = coef_ref[b].astype(F32)
                rest = [coef[packed:, at : at + free] for at in range(0, mus, free)]
                rest = jnp.concatenate(rest, axis=0)
                rest_ref[b] = jnp.concatenate([jnp.zeros((rest.shape[0], cols), F32), rest], axis=1)
                for x in range(side):
                    out_ref[b * side + x, :, :mus] = coef[:packed].astype(BF16)
    halves = []
    for x in range(side):
        half = half_ref[x]
        rest = [jnp.zeros((mus // free * last, free), F32)]
        rest += [half[packed:, at : at + free] for at in range(0, cols, free)]
        rest.append(jnp.zeros((packed - (mus + cols) // free * last, free), F32))
        halves.append(jnp.concatenate([half[:packed, :cols], jnp.concatenate(rest, axis=0)], axis=1))
    for x in range(side):
        low = halves[x][mus // free * last :].astype(BF16)
        for b in range(blocks):
            high = (halves[x][: mus // free * last] + rest_ref[b]).astype(BF16)
            out_ref[b * side + x, :, mus:] = jnp.concatenate([high, low], axis=0)


def amp_of(nuw, few, half, coef):
    depth, mus = coef.shape
    every = mus * nuw
    width = half.shape[1]
    amp = lax.dot_general(coef, half, ROWS, preferred_element_type=F32).astype(BF16)
    wide = mm(ones_where(div(row_ids(every), nuw) == lane_ids(mus)), amp)
    own = mod(row_ids(every), nuw) == div(lane_ids(width), few)
    wide = jnp.where(own, wide, 0.0).astype(BF16)
    pick = ones_where(row_ids(2 * few) == mod(lane_ids(width), few))
    return lax.dot_general(pick, wide, LANES, preferred_element_type=F32)[:few].astype(BF16)


def unpack_kernel(cols, last, in_ref, coef_ref, half_ref):
    parts, packed, lanes = in_ref.shape
    mus = lanes // 2
    free = mus - cols
    whole = in_ref[...].astype(F32)
    rest = whole[:, :, mus + cols :]
    none = jnp.zeros((parts, coef_ref.shape[1] - packed - last, mus), F32)
    count = mus // free
    coef = [rest[:, i * last : (i + 1) * last] for i in range(count)]
    coef = jnp.concatenate([whole[:, :, :mus], jnp.concatenate(coef, axis=2), none], axis=1)
    coef_ref[...] = coef.astype(BF16)
    half = [rest[:, i * last : (i + 1) * last] for i in range(count, count + cols // free)]
    half.append(jnp.zeros((parts, last, free), F32))
    half = jnp.concatenate([whole[:, :, mus:], jnp.concatenate(half, axis=2), none], axis=1)
    half_ref[...] = half.astype(BF16)


def own_amp_kernel(nuw, half_ref, coef_ref, out_ref):
    parts, padded, mus = coef_ref.shape
    coef = coef_ref[...].reshape(parts * padded, mus)
    half = half_ref[...].reshape(parts * padded, mus)
    out_ref[...] = amp_of(nuw, out_ref.shape[0], half, coef)


def amp_kernel(nuw, core_ref, half_ref, coef_ref, own_ref, out_ref):
    parts, padded, mus = coef_ref.shape
    dests, few, cols = out_ref.shape
    repeat = dests * cols // (2 * mus * nuw)
    blocks = dests // (2 * repeat)
    half = half_ref[...].reshape(parts * padded, mus)
    other_amp = amp_of(nuw, few, half, coef_ref[...].reshape(parts * padded, mus))
    for other, amp in enumerate([own_ref[...], other_amp]):
        for b in range(blocks):
            for zh in range(repeat):
                dest = ((core_ref[0] ^ other) * blocks + b) * repeat + zh
                out_ref[dest] = amp[:, b * cols : (b + 1) * cols]


def terms_kernel(blk, mask_ref, core_ref, amp_ref, other_amp_ref, ints_ref, out_ref, all_ref):
    rows, cols = ints_ref.shape
    dests, few, _ = out_ref.shape
    half = amp_ref.shape[0]
    side = 4
    at = pl.multiple_of(core_ref[0] * half, half)
    all_ref[pl.ds(at, half), :] = amp_ref[...]
    at = pl.multiple_of((core_ref[0] ^ 1) * half, half)
    all_ref[pl.ds(at, half), :] = other_amp_ref[...]
    for col in range(cols // blk):
        total = None
        for row in range(rows // blk):
            keep = mask_ref[row, col].astype(F32)
            term = keep * mm(
                all_ref[:, row * blk : (row + 1) * blk],
                ints_ref[row * blk : (row + 1) * blk, col * blk : (col + 1) * blk],
            )
            total = term if total is None else total + term
        for dest in range(dests):
            o, x = dest // side, dest % side
            at = o % 2 * half + x * (half // side) + o // 2 * few
            out_ref[dest, :, col * blk : (col + 1) * blk] = total[at : at + few].astype(BF16)


def sum_terms_kernel(in_ref, out_ref):
    total = in_ref[0].astype(F32)
    for part in range(1, in_ref.shape[0]):
        total = total + in_ref[part].astype(F32)
    out_ref[...] = total.astype(BF16)


def forward_kernel(nuw, last, core_ref, coef_ref, other_coef_ref, lad_ref, out_ref, order_ref):
    dests, packed, lanes = out_ref.shape
    padded = coef_ref.shape[1]
    few, cols = lad_ref.shape
    mus = cols // nuw // 2
    part_cols = 384
    run = part_cols // nuw
    row = row_ids(lanes)
    source = jnp.where(row < nuw * few, mod(row, few), -1)
    wide = mm(ones_where(source == lane_ids(few)), lad_ref[...])
    own = div(row, few) == mod(lane_ids(part_cols), nuw)
    collect = ones_where(div(lane_ids(part_cols), nuw) == row_ids(run))
    for part in range(cols // part_cols):
        some = wide[:, part * part_cols : (part + 1) * part_cols]
        some = jnp.where(own, some, 0.0).astype(BF16)
        some = lax.dot_general(collect, some, LANES, preferred_element_type=F32)
        order_ref[part * run : (part + 1) * run, :] = some.astype(BF16)
    fwd = None
    for other in range(2):
        coef = (other_coef_ref if other else coef_ref)[...]
        start = pl.multiple_of((core_ref[0] ^ other) * mus, mus)
        part = mm(coef.reshape(dests * padded, mus), order_ref[pl.ds(start, mus), :])
        fwd = part if fwd is None else fwd + part
    fwd = fwd.reshape(dests, padded, lanes)
    used = nuw * few
    free = lanes - used
    rest = [fwd[:, packed : packed + last, at : at + free] for at in range(0, used, free)]
    rest.append(jnp.zeros((dests, packed - len(rest) * last, free), F32))
    fwd = jnp.concatenate([fwd[:, :packed, :used], jnp.concatenate(rest, axis=1)], axis=2)
    out_ref[...] = fwd.astype(BF16)


def out_kernel(steps, few, fwd_ref, win_ref, out_hbm, out_ref, sems):
    parts, packed, lanes = fwd_ref.shape
    total, pairs, nv = out_ref.shape
    last = total - packed
    used = win_ref.shape[0] * few
    free = lanes - used
    side = pairs // few
    virt = total // steps
    win = repeated(win_ref[...], few, lanes)
    own = row_ids(few) == mod(lane_ids(lanes), few)
    fwds = []
    for x in range(side):
        fwd = None
        for block in range(parts // side):
            part = fwd_ref[block * side + x].astype(F32)
            fwd = part if fwd is None else fwd + part
        rest = [fwd[i * last : (i + 1) * last, used:] for i in range(used // free)]
        rest.append(jnp.zeros((last, free), F32))
        fwds.append(jnp.concatenate([fwd, jnp.concatenate(rest, axis=1)], axis=0))
    copies = []
    for step in range(steps):
        cut = slice(step * virt, (step + 1) * virt)
        wide = [jnp.broadcast_to(fwd[cut][:, None, :], (virt, few, lanes)) for fwd in fwds]
        wide = jnp.concatenate([jnp.where(own, part, 0.0) for part in wide], axis=1)
        wide = wide.reshape(virt * pairs, lanes).astype(BF16)
        out_ref[cut] = mm(wide, win).astype(BF16).reshape(virt, pairs, nv)
        copies.append(pltpu.make_async_copy(out_ref.at[cut], out_hbm.at[cut], sems.at[step]))
        copies[-1].start()
    for copy in copies:
        copy.wait()


def params(mib=24):
    return pltpu.CompilerParams(vmem_limit_bytes=mib * 1024 * 1024)


def swap(array, axis):
    return lax.ppermute(array, axis, [(0, 1), (1, 0)])


def turn(array, sizes):
    square = sizes["y"] * sizes["z"]
    pairs = [(one, one % square * square + one // square) for one in range(square * square)]
    return lax.ppermute(array, ("y", "z", "zh", "core"), pairs)


def exchange(array, axes):
    return lax.all_to_all(array, axes, split_axis=0, concat_axis=0, tiled=True)


def local(sizes, amplitudes, window_coef, virtual_coef, integrals, block_mask):
    pairs, virt, _ = amplitudes.shape
    nuw, nv = window_coef.shape
    nao = virtual_coef.shape[0]
    rows, cols = integrals.shape
    side = sizes["y"]
    sp = side * sizes["z"] * sizes["x"]
    op = sizes["zh"] * sizes["core"]
    few = pairs // side
    mus = nao * side // sp
    width = 128
    steps = 4
    padded, packed = -(-virt // 16) * 16, virt // 8 * 8
    amp = jnp.transpose(amplitudes, (1, 0, 2))
    coef = jnp.transpose(virtual_coef, (1, 0))
    my_core = lax.axis_index("core").reshape(1)
    smem = pl.BlockSpec(memory_space=pltpu.SMEM)
    hbm = pl.BlockSpec(memory_space=pltpu.HBM)
    vmem = pl.BlockSpec(memory_space=pltpu.VMEM)

    sent = pl.pallas_call(
        functools.partial(half_kernel, steps, few),
        in_specs=[smem, hbm, hbm, hbm],
        out_specs=vmem,
        out_shape=jax.ShapeDtypeStruct((sp, packed, mus // 2 + width), BF16),
        scratch_shapes=[
            pltpu.VMEM((virt, pairs, nv), BF16),
            pltpu.VMEM((nuw, nv), BF16),
            pltpu.VMEM((nao // mus, virt, mus // 2), BF16),
            pltpu.VMEM((side, virt, width), F32),
            pltpu.VMEM((nao // mus, 16, width), F32),
            pltpu.SemaphoreType.DMA((steps + 1 + nao // mus,)),
        ],
        compiler_params=params(54),
        name="half",
    )(my_core, amp, window_coef, coef)
    chunk = exchange(sent, ("y", "z", "x"))
    own_coef, half = pl.pallas_call(
        functools.partial(unpack_kernel, nuw * few, virt - packed),
        out_shape=[jax.ShapeDtypeStruct((sp, padded, width), BF16)] * 2,
        compiler_params=params(),
        name="unpack",
    )(chunk)
    other_coef = swap(own_coef, "core")
    flat = sizes["x"] * sizes["zh"]
    own_amp = pl.pallas_call(
        functools.partial(own_amp_kernel, nuw),
        out_shape=jax.ShapeDtypeStruct((few, mus // 2 * nuw), BF16),
        compiler_params=params(),
        name="own_amp",
    )(half, own_coef)
    ao_amp = pl.pallas_call(
        functools.partial(amp_kernel, nuw),
        in_specs=[smem, vmem, vmem, vmem],
        out_specs=vmem,
        out_shape=jax.ShapeDtypeStruct((flat, few, rows), BF16),
        compiler_params=params(),
        name="amp",
    )(my_core, half, other_coef, own_amp)
    amp_here = exchange(ao_amp, ("x", "zh")).reshape(flat * few, rows)
    amp_there = swap(amp_here, "core")

    terms = pl.pallas_call(
        functools.partial(terms_kernel, rows // block_mask.shape[0]),
        in_specs=[smem, smem, vmem, vmem, vmem],
        out_specs=vmem,
        out_shape=jax.ShapeDtypeStruct((sp, few, cols), BF16),
        scratch_shapes=[pltpu.VMEM((op * pairs, rows), BF16)],
        compiler_params=params(),
        name="terms",
    )(block_mask, my_core, amp_here, amp_there, integrals)
    pieces = exchange(terms, ("y", "z", "x"))
    ladder = pl.pallas_call(
        sum_terms_kernel,
        out_shape=jax.ShapeDtypeStruct((few, cols), BF16),
        compiler_params=params(),
        name="sum_terms",
    )(pieces)
    owned = turn(ladder, sizes)
    fwd = pl.pallas_call(
        functools.partial(forward_kernel, nuw, virt - packed),
        in_specs=[smem, vmem, vmem, vmem],
        out_specs=vmem,
        out_shape=jax.ShapeDtypeStruct((sp, packed, width), BF16),
        scratch_shapes=[pltpu.VMEM((mus, width), BF16)],
        compiler_params=params(),
        name="forward",
    )(my_core, own_coef, other_coef, owned)
    fwd = exchange(fwd, ("y", "z", "x"))
    out = pl.pallas_call(
        functools.partial(out_kernel, steps, few),
        in_specs=[vmem, vmem],
        out_specs=hbm,
        out_shape=jax.ShapeDtypeStruct((virt, pairs, nv), BF16),
        scratch_shapes=[pltpu.VMEM((virt, pairs, nv), BF16), pltpu.SemaphoreType.DMA((steps,))],
        compiler_params=params(),
        name="out",
    )(fwd, window_coef)
    return jnp.transpose(out, (1, 0, 2))


def solution(mesh):
    sizes = {"y": 4, "z": 2, "x": 4, "zh": 4, "core": 2}
    fine = Mesh(mesh.devices.reshape(tuple(sizes.values())), tuple(sizes))
    sp, op = ("y", "z", "x"), ("zh", "core")
    placed = (P(op, sp, None), P(), P(None, sp), P(sp, op), P(sp, op))
    return jax.shard_map(
        functools.partial(local, sizes),
        mesh=fine,
        in_specs=placed,
        out_specs=P(op, sp, None),
        check_vma=False,
    )
```

```python
import functools

import jax
import jax.numpy as jnp
from jax import lax
from jax.experimental import pallas as pl
from jax.experimental.pallas import tpu as pltpu
from jax.sharding import Mesh
from jax.sharding import PartitionSpec as P

F32 = jnp.float32
BF16 = jnp.bfloat16
ROWS = (((0,), (0,)), ((), ()))
LANES = (((1,), (1,)), ((), ()))


def iota(shape, dim):
    return lax.broadcasted_iota(jnp.int32, shape, dim)


def div(x, n):
    if n & (n - 1) == 0:
        return lax.shift_right_logical(x, n.bit_length() - 1)
    return lax.shift_right_logical(x * ((1 << 19) // n + 1), 19)


def mod(x, n):
    return x & (n - 1) if n & (n - 1) == 0 else x - div(x, n) * n


def row_ids(size):
    return iota((size, 1), 0)


def lane_ids(size):
    return iota((1, size), 1)


def ones_where(cond):
    return jnp.where(cond, 1.0, 0.0).astype(BF16)


def mm(x, y):
    return jnp.dot(x, y, preferred_element_type=F32)


def repeated(win, few, width):
    nuw, nv = win.shape
    win = jnp.broadcast_to(win.astype(F32)[:, None, :], (nuw, few, nv)).reshape(nuw * few, nv)
    return jnp.concatenate([win, jnp.zeros((width - nuw * few, nv), F32)], axis=0).astype(BF16)


def half_kernel(
    steps, few, core_ref, amp_hbm, win_hbm, coef_hbm, out_ref, amp_ref, win_ref, coef_ref, half_ref, rest_ref, sems
):
    total, pairs, _ = amp_hbm.shape
    dests, both, width = out_ref.shape
    blocks, _, mus = coef_ref.shape
    packed = both // 2
    side = pairs // few
    last = total - packed
    cols = win_hbm.shape[0] * few
    free = width - cols
    virt = total // steps
    rows = virt * pairs
    ahead = 3
    copies = [
        pltpu.make_async_copy(
            amp_hbm.at[step * virt : (step + 1) * virt],
            amp_ref.at[step * virt : (step + 1) * virt],
            sems.at[step],
        )
        for step in range(steps)
    ]
    win_copy = pltpu.make_async_copy(win_hbm, win_ref, sems.at[steps])
    coef_copies = []
    for b in range(blocks):
        start = pl.multiple_of((2 * b + core_ref[0]) * mus, mus)
        coef_copies.append(
            pltpu.make_async_copy(coef_hbm.at[:, pl.ds(start, mus)], coef_ref.at[b], sems.at[steps + 1 + b])
        )
    win_copy.start()
    for copy in copies[:ahead]:
        copy.start()
    for copy in coef_copies:
        copy.start()
    win_copy.wait()
    win = repeated(win_ref[...], few, width)
    own = mod(row_ids(few), few) == mod(lane_ids(width), few)
    for step in range(steps):
        copies[step].wait()
        if step + ahead < steps:
            copies[step + ahead].start()
        block = amp_ref[step * virt : (step + 1) * virt].reshape(rows, amp_ref.shape[2])
        half = lax.dot_general(block, win, LANES, preferred_element_type=F32)
        half = half.astype(BF16).astype(F32).reshape(virt, side, few, width)
        for x in range(side):
            part = jnp.sum(jnp.where(own, half[:, x], 0.0), axis=1)
            half_ref[x, step * virt : (step + 1) * virt, :] = part
        if step == 0:
            for b in range(blocks):
                coef_copies[b].wait()
                coef = coef_ref[b].astype(F32)
                rest = [coef[packed:, at : at + free] for at in range(0, mus, free)]
                rest = jnp.concatenate(rest, axis=0)
                rest = jnp.concatenate([jnp.zeros((rest.shape[0], cols), F32), rest], axis=1)
                rest_ref[b, :packed] = coef[:packed]
                rest_ref[b, packed:] = rest
    halves = []
    for x in range(side):
        half = half_ref[x]
        rest = [jnp.zeros((mus // free * last, free), F32)]
        rest += [half[packed:, at : at + free] for at in range(0, cols, free)]
        rest.append(jnp.zeros((packed - (mus + cols) // free * last, free), F32))
        halves.append(jnp.concatenate([half[:packed, :cols], jnp.concatenate(rest, axis=0)], axis=1))
    high = mus // free * last
    for b in range(blocks):
        coef = rest_ref[b]
        for x in range(side):
            piece = [coef[:packed], coef[packed:] + halves[x][:high], halves[x][high:]]
            out_ref[b * side + x] = jnp.concatenate(piece, axis=0).astype(BF16)


def amp_of(nuw, few, half, coef):
    depth, mus = coef.shape
    every = mus * nuw
    width = half.shape[1]
    amp = lax.dot_general(coef, half, ROWS, preferred_element_type=F32).astype(BF16)
    wide = mm(ones_where(div(row_ids(every), nuw) == lane_ids(mus)), amp)
    own = mod(row_ids(every), nuw) == div(lane_ids(width), few)
    wide = jnp.where(own, wide, 0.0).astype(BF16)
    pick = ones_where(row_ids(2 * few) == mod(lane_ids(width), few))
    return lax.dot_general(pick, wide, LANES, preferred_element_type=F32)[:few].astype(BF16)


def unpack_kernel(cols, last, in_ref, coef_ref, half_ref):
    parts, both, mus = in_ref.shape
    packed = both // 2
    free = mus - cols
    whole = in_ref[...].astype(F32)
    rest = whole[:, packed:, cols:]
    none = jnp.zeros((parts, coef_ref.shape[1] - packed - last, mus), F32)
    count = mus // free
    coef = [rest[:, i * last : (i + 1) * last] for i in range(count)]
    coef = jnp.concatenate([whole[:, :packed], jnp.concatenate(coef, axis=2), none], axis=1)
    coef_ref[...] = coef.astype(BF16)
    half = [rest[:, i * last : (i + 1) * last] for i in range(count, count + cols // free)]
    half.append(jnp.zeros((parts, last, free), F32))
    half = jnp.concatenate([whole[:, packed:], jnp.concatenate(half, axis=2), none], axis=1)
    half_ref[...] = half.astype(BF16)


def own_amp_kernel(nuw, half_ref, coef_ref, out_ref):
    parts, padded, mus = coef_ref.shape
    coef = coef_ref[...].reshape(parts * padded, mus)
    half = half_ref[...].reshape(parts * padded, mus)
    out_ref[...] = amp_of(nuw, out_ref.shape[0], half, coef)


def amp_kernel(nuw, core_ref, half_ref, coef_ref, own_ref, out_ref):
    parts, padded, mus = coef_ref.shape
    dests, few, cols = out_ref.shape
    repeat = dests * cols // (2 * mus * nuw)
    blocks = dests // (2 * repeat)
    half = half_ref[...].reshape(parts * padded, mus)
    other_amp = amp_of(nuw, few, half, coef_ref[...].reshape(parts * padded, mus))
    for other, amp in enumerate([own_ref[...], other_amp]):
        for b in range(blocks):
            for zh in range(repeat):
                dest = ((core_ref[0] ^ other) * blocks + b) * repeat + zh
                out_ref[dest] = amp[:, b * cols : (b + 1) * cols]


def terms_kernel(blk, mask_ref, core_ref, amp_ref, other_amp_ref, ints_ref, out_ref, all_ref):
    rows, cols = ints_ref.shape
    dests, few, _ = out_ref.shape
    half = amp_ref.shape[0]
    side = 4
    at = pl.multiple_of(core_ref[0] * half, half)
    all_ref[pl.ds(at, half), :] = amp_ref[...]
    at = pl.multiple_of((core_ref[0] ^ 1) * half, half)
    all_ref[pl.ds(at, half), :] = other_amp_ref[...]
    for col in range(cols // blk):
        total = None
        for row in range(rows // blk):
            keep = mask_ref[row, col].astype(F32)
            term = keep * mm(
                all_ref[:, row * blk : (row + 1) * blk],
                ints_ref[row * blk : (row + 1) * blk, col * blk : (col + 1) * blk],
            )
            total = term if total is None else total + term
        for dest in range(dests):
            o, x = dest // side, dest % side
            at = o % 2 * half + x * (half // side) + o // 2 * few
            out_ref[dest, :, col * blk : (col + 1) * blk] = total[at : at + few].astype(BF16)


def sum_terms_kernel(in_ref, out_ref):
    total = in_ref[0].astype(F32)
    for part in range(1, in_ref.shape[0]):
        total = total + in_ref[part].astype(F32)
    out_ref[...] = total.astype(BF16)


def forward_kernel(nuw, last, core_ref, coef_ref, other_coef_ref, lad_ref, out_ref, order_ref):
    dests, packed, lanes = out_ref.shape
    padded = coef_ref.shape[1]
    few, cols = lad_ref.shape
    mus = cols // nuw // 2
    part_cols = 384
    run = part_cols // nuw
    row = row_ids(lanes)
    source = jnp.where(row < nuw * few, mod(row, few), -1)
    wide = mm(ones_where(source == lane_ids(few)), lad_ref[...])
    own = div(row, few) == mod(lane_ids(part_cols), nuw)
    collect = ones_where(div(lane_ids(part_cols), nuw) == row_ids(run))
    for part in range(cols // part_cols):
        some = wide[:, part * part_cols : (part + 1) * part_cols]
        some = jnp.where(own, some, 0.0).astype(BF16)
        some = lax.dot_general(collect, some, LANES, preferred_element_type=F32)
        order_ref[part * run : (part + 1) * run, :] = some.astype(BF16)
    fwd = None
    for other in range(2):
        coef = (other_coef_ref if other else coef_ref)[...]
        start = pl.multiple_of((core_ref[0] ^ other) * mus, mus)
        part = mm(coef.reshape(dests * padded, mus), order_ref[pl.ds(start, mus), :])
        fwd = part if fwd is None else fwd + part
    fwd = fwd.reshape(dests, padded, lanes)
    used = nuw * few
    free = lanes - used
    rest = [fwd[:, packed : packed + last, at : at + free] for at in range(0, used, free)]
    rest.append(jnp.zeros((dests, packed - len(rest) * last, free), F32))
    fwd = jnp.concatenate([fwd[:, :packed, :used], jnp.concatenate(rest, axis=1)], axis=2)
    out_ref[...] = fwd.astype(BF16)


def out_kernel(steps, few, fwd_ref, win_ref, out_hbm, out_ref, sems):
    parts, packed, lanes = fwd_ref.shape
    total, pairs, nv = out_ref.shape
    last = total - packed
    used = win_ref.shape[0] * few
    free = lanes - used
    side = pairs // few
    virt = total // steps
    win = repeated(win_ref[...], few, lanes)
    own = row_ids(few) == mod(lane_ids(lanes), few)
    fwds = []
    for x in range(side):
        fwd = None
        for block in range(parts // side):
            part = fwd_ref[block * side + x].astype(F32)
            fwd = part if fwd is None else fwd + part
        rest = [fwd[i * last : (i + 1) * last, used:] for i in range(used // free)]
        rest.append(jnp.zeros((last, free), F32))
        fwds.append(jnp.concatenate([fwd, jnp.concatenate(rest, axis=1)], axis=0))
    copies = []
    for step in range(steps):
        cut = slice(step * virt, (step + 1) * virt)
        wide = [jnp.broadcast_to(fwd[cut][:, None, :], (virt, few, lanes)) for fwd in fwds]
        wide = jnp.concatenate([jnp.where(own, part, 0.0) for part in wide], axis=1)
        wide = wide.reshape(virt * pairs, lanes).astype(BF16)
        out_ref[cut] = mm(wide, win).astype(BF16).reshape(virt, pairs, nv)
        copies.append(pltpu.make_async_copy(out_ref.at[cut], out_hbm.at[cut], sems.at[step]))
        copies[-1].start()
    for copy in copies:
        copy.wait()


def params(mib=24):
    return pltpu.CompilerParams(vmem_limit_bytes=mib * 1024 * 1024)


def swap(array, axis):
    return lax.ppermute(array, axis, [(0, 1), (1, 0)])


def turn(array, sizes):
    square = sizes["y"] * sizes["z"]
    pairs = [(one, one % square * square + one // square) for one in range(square * square)]
    return lax.ppermute(array, ("y", "z", "zh", "core"), pairs)


def exchange(array, axes):
    return lax.all_to_all(array, axes, split_axis=0, concat_axis=0, tiled=True)


def local(sizes, amplitudes, window_coef, virtual_coef, integrals, block_mask):
    pairs, virt, _ = amplitudes.shape
    nuw, nv = window_coef.shape
    nao = virtual_coef.shape[0]
    rows, cols = integrals.shape
    side = sizes["y"]
    sp = side * sizes["z"] * sizes["x"]
    op = sizes["zh"] * sizes["core"]
    few = pairs // side
    mus = nao * side // sp
    width = 128
    steps = 4
    padded, packed = -(-virt // 16) * 16, virt // 8 * 8
    amp = jnp.transpose(amplitudes, (1, 0, 2))
    coef = jnp.transpose(virtual_coef, (1, 0))
    my_core = lax.axis_index("core").reshape(1)
    smem = pl.BlockSpec(memory_space=pltpu.SMEM)
    hbm = pl.BlockSpec(memory_space=pltpu.HBM)
    vmem = pl.BlockSpec(memory_space=pltpu.VMEM)

    sent = pl.pallas_call(
        functools.partial(half_kernel, steps, few),
        in_specs=[smem, hbm, hbm, hbm],
        out_specs=vmem,
        out_shape=jax.ShapeDtypeStruct((sp, 2 * packed, width), BF16),
        scratch_shapes=[
            pltpu.VMEM((virt, pairs, nv), BF16),
            pltpu.VMEM((nuw, nv), BF16),
            pltpu.VMEM((nao // mus, virt, mus // 2), BF16),
            pltpu.VMEM((side, virt, width), F32),
            pltpu.VMEM((nao // mus, packed + 16, width), F32),
            pltpu.SemaphoreType.DMA((steps + 1 + nao // mus,)),
        ],
        compiler_params=params(54),
        name="half",
    )(my_core, amp, window_coef, coef)
    chunk = exchange(sent, ("y", "z", "x"))
    own_coef, half = pl.pallas_call(
        functools.partial(unpack_kernel, nuw * few, virt - packed),
        out_shape=[jax.ShapeDtypeStruct((sp, padded, width), BF16)] * 2,
        compiler_params=params(),
        name="unpack",
    )(chunk)
    other_coef = swap(own_coef, "core")
    flat = sizes["x"] * sizes["zh"]
    own_amp = pl.pallas_call(
        functools.partial(own_amp_kernel, nuw),
        out_shape=jax.ShapeDtypeStruct((few, mus // 2 * nuw), BF16),
        compiler_params=params(),
        name="own_amp",
    )(half, own_coef)
    ao_amp = pl.pallas_call(
        functools.partial(amp_kernel, nuw),
        in_specs=[smem, vmem, vmem, vmem],
        out_specs=vmem,
        out_shape=jax.ShapeDtypeStruct((flat, few, rows), BF16),
        compiler_params=params(),
        name="amp",
    )(my_core, half, other_coef, own_amp)
    amp_here = exchange(ao_amp, ("x", "zh")).reshape(flat * few, rows)
    amp_there = swap(amp_here, "core")

    terms = pl.pallas_call(
        functools.partial(terms_kernel, rows // block_mask.shape[0]),
        in_specs=[smem, smem, vmem, vmem, vmem],
        out_specs=vmem,
        out_shape=jax.ShapeDtypeStruct((sp, few, cols), BF16),
        scratch_shapes=[pltpu.VMEM((op * pairs, rows), BF16)],
        compiler_params=params(),
        name="terms",
    )(block_mask, my_core, amp_here, amp_there, integrals)
    pieces = exchange(terms, ("y", "z", "x"))
    ladder = pl.pallas_call(
        sum_terms_kernel,
        out_shape=jax.ShapeDtypeStruct((few, cols), BF16),
        compiler_params=params(),
        name="sum_terms",
    )(pieces)
    owned = turn(ladder, sizes)
    fwd = pl.pallas_call(
        functools.partial(forward_kernel, nuw, virt - packed),
        in_specs=[smem, vmem, vmem, vmem],
        out_specs=vmem,
        out_shape=jax.ShapeDtypeStruct((sp, packed, width), BF16),
        scratch_shapes=[pltpu.VMEM((mus, width), BF16)],
        compiler_params=params(),
        name="forward",
    )(my_core, own_coef, other_coef, owned)
    fwd = exchange(fwd, ("y", "z", "x"))
    out = pl.pallas_call(
        functools.partial(out_kernel, steps, few),
        in_specs=[vmem, vmem],
        out_specs=hbm,
        out_shape=jax.ShapeDtypeStruct((virt, pairs, nv), BF16),
        scratch_shapes=[pltpu.VMEM((virt, pairs, nv), BF16), pltpu.SemaphoreType.DMA((steps,))],
        compiler_params=params(),
        name="out",
    )(fwd, window_coef)
    return jnp.transpose(out, (1, 0, 2))


def solution(mesh):
    sizes = {"y": 4, "z": 2, "x": 4, "zh": 4, "core": 2}
    fine = Mesh(mesh.devices.reshape(tuple(sizes.values())), tuple(sizes))
    sp, op = ("y", "z", "x"), ("zh", "core")
    placed = (P(op, sp, None), P(), P(None, sp), P(sp, op), P(sp, op))
    return jax.shard_map(
        functools.partial(local, sizes),
        mesh=fine,
        in_specs=placed,
        out_specs=P(op, sp, None),
        check_vma=False,
    )
```

```python
import functools

import jax
import jax.numpy as jnp
from jax import lax
from jax.experimental import pallas as pl
from jax.experimental.pallas import tpu as pltpu
from jax.sharding import Mesh
from jax.sharding import PartitionSpec as P

F32 = jnp.float32
BF16 = jnp.bfloat16
ROWS = (((0,), (0,)), ((), ()))
LANES = (((1,), (1,)), ((), ()))


def iota(shape, dim):
    return lax.broadcasted_iota(jnp.int32, shape, dim)


def div(x, n):
    if n & (n - 1) == 0:
        return lax.shift_right_logical(x, n.bit_length() - 1)
    return lax.shift_right_logical(x * ((1 << 19) // n + 1), 19)


def mod(x, n):
    return x & (n - 1) if n & (n - 1) == 0 else x - div(x, n) * n


def row_ids(size):
    return iota((size, 1), 0)


def lane_ids(size):
    return iota((1, size), 1)


def ones_where(cond):
    return jnp.where(cond, 1.0, 0.0).astype(BF16)


def mm(x, y):
    return jnp.dot(x, y, preferred_element_type=F32)


def repeated(win, few, width):
    nuw, nv = win.shape
    win = jnp.broadcast_to(win.astype(F32)[:, None, :], (nuw, few, nv)).reshape(nuw * few, nv)
    return jnp.concatenate([win, jnp.zeros((width - nuw * few, nv), F32)], axis=0).astype(BF16)


def half_kernel(
    steps, few, core_ref, amp_hbm, win_hbm, coef_hbm, out_ref, amp_ref, win_ref, coef_ref, half_ref, rest_ref, sems
):
    total, pairs, _ = amp_hbm.shape
    dests, both, width = out_ref.shape
    blocks, _, mus = coef_ref.shape
    packed = both // 2
    side = pairs // few
    last = total - packed
    cols = win_hbm.shape[0] * few
    free = width - cols
    virt = total // steps
    rows = virt * pairs
    ahead = 3
    copies = [
        pltpu.make_async_copy(
            amp_hbm.at[step * virt : (step + 1) * virt],
            amp_ref.at[step * virt : (step + 1) * virt],
            sems.at[step],
        )
        for step in range(steps)
    ]
    win_copy = pltpu.make_async_copy(win_hbm, win_ref, sems.at[steps])
    coef_copies = []
    for b in range(blocks):
        start = pl.multiple_of((2 * b + core_ref[0]) * mus, mus)
        coef_copies.append(
            pltpu.make_async_copy(coef_hbm.at[:, pl.ds(start, mus)], coef_ref.at[b], sems.at[steps + 1 + b])
        )
    for copy in coef_copies:
        copy.start()
    win_copy.start()
    for copy in copies[:ahead]:
        copy.start()
    high = mus // free * last
    whole = packed // 16 * 16
    for b in range(blocks):
        coef_copies[b].wait()
        coef = coef_ref[b].astype(F32)
        rest = [coef[packed:, at : at + free] for at in range(0, mus, free)]
        rest = jnp.concatenate(rest, axis=0)
        rest = jnp.concatenate([jnp.zeros((high, cols), F32), rest], axis=1)
        rest_ref[b] = jnp.concatenate([coef[whole:packed], rest], axis=0)
        for x in range(side):
            out_ref[b * side + x, :whole] = coef[:whole].astype(BF16)
    win_copy.wait()
    win = repeated(win_ref[...], few, width)
    own = mod(row_ids(few), few) == mod(lane_ids(width), few)
    for step in range(steps):
        copies[step].wait()
        if step + ahead < steps:
            copies[step + ahead].start()
        block = amp_ref[step * virt : (step + 1) * virt].reshape(rows, amp_ref.shape[2])
        half = lax.dot_general(block, win, LANES, preferred_element_type=F32)
        half = half.astype(BF16).astype(F32).reshape(virt, side, few, width)
        for x in range(side):
            part = jnp.sum(jnp.where(own, half[:, x], 0.0), axis=1)
            half_ref[x, step * virt : (step + 1) * virt, :] = part
    halves = []
    for x in range(side):
        half = half_ref[x]
        rest = [jnp.zeros((mus // free * last, free), F32)]
        rest += [half[packed:, at : at + free] for at in range(0, cols, free)]
        rest.append(jnp.zeros((packed - (mus + cols) // free * last, free), F32))
        halves.append(jnp.concatenate([half[:packed, :cols], jnp.concatenate(rest, axis=0)], axis=1))
    left = packed - whole
    middle = high + left
    for x in range(side):
        low = halves[x][middle:].astype(BF16)
        for b in range(blocks):
            rest = rest_ref[b]
            piece = [rest[:left], rest[left:] + halves[x][:high], halves[x][high:middle]]
            piece = jnp.concatenate(piece, axis=0).astype(BF16)
            out_ref[b * side + x, whole : packed + middle] = piece
            out_ref[b * side + x, packed + middle :] = low


def amp_of(nuw, few, half, coef):
    depth, mus = coef.shape
    every = mus * nuw
    width = half.shape[1]
    amp = lax.dot_general(coef, half, ROWS, preferred_element_type=F32).astype(BF16)
    wide = mm(ones_where(div(row_ids(every), nuw) == lane_ids(mus)), amp)
    own = mod(row_ids(every), nuw) == div(lane_ids(width), few)
    wide = jnp.where(own, wide, 0.0).astype(BF16)
    pick = ones_where(row_ids(2 * few) == mod(lane_ids(width), few))
    return lax.dot_general(pick, wide, LANES, preferred_element_type=F32)[:few].astype(BF16)


def unpack_kernel(cols, last, in_ref, coef_ref, half_ref):
    parts, both, mus = in_ref.shape
    packed = both // 2
    free = mus - cols
    whole = in_ref[...].astype(F32)
    rest = whole[:, packed:, cols:]
    none = jnp.zeros((parts, coef_ref.shape[1] - packed - last, mus), F32)
    count = mus // free
    coef = [rest[:, i * last : (i + 1) * last] for i in range(count)]
    coef = jnp.concatenate([whole[:, :packed], jnp.concatenate(coef, axis=2), none], axis=1)
    coef_ref[...] = coef.astype(BF16)
    half = [rest[:, i * last : (i + 1) * last] for i in range(count, count + cols // free)]
    half.append(jnp.zeros((parts, last, free), F32))
    half = jnp.concatenate([whole[:, packed:], jnp.concatenate(half, axis=2), none], axis=1)
    half_ref[...] = half.astype(BF16)


def own_amp_kernel(nuw, half_ref, coef_ref, out_ref):
    parts, padded, mus = coef_ref.shape
    coef = coef_ref[...].reshape(parts * padded, mus)
    half = half_ref[...].reshape(parts * padded, mus)
    out_ref[...] = amp_of(nuw, out_ref.shape[0], half, coef)


def amp_kernel(nuw, core_ref, half_ref, coef_ref, own_ref, out_ref):
    parts, padded, mus = coef_ref.shape
    dests, few, cols = out_ref.shape
    repeat = dests * cols // (2 * mus * nuw)
    blocks = dests // (2 * repeat)
    half = half_ref[...].reshape(parts * padded, mus)
    other_amp = amp_of(nuw, few, half, coef_ref[...].reshape(parts * padded, mus))
    for other, amp in enumerate([own_ref[...], other_amp]):
        for b in range(blocks):
            for zh in range(repeat):
                dest = ((core_ref[0] ^ other) * blocks + b) * repeat + zh
                out_ref[dest] = amp[:, b * cols : (b + 1) * cols]


def terms_kernel(blk, mask_ref, core_ref, amp_ref, other_amp_ref, ints_ref, out_ref, all_ref):
    rows, cols = ints_ref.shape
    dests, few, _ = out_ref.shape
    half = amp_ref.shape[0]
    side = 4
    at = pl.multiple_of(core_ref[0] * half, half)
    all_ref[pl.ds(at, half), :] = amp_ref[...]
    at = pl.multiple_of((core_ref[0] ^ 1) * half, half)
    all_ref[pl.ds(at, half), :] = other_amp_ref[...]
    for col in range(cols // blk):
        total = None
        for row in range(rows // blk):
            keep = mask_ref[row, col].astype(F32)
            term = keep * mm(
                all_ref[:, row * blk : (row + 1) * blk],
                ints_ref[row * blk : (row + 1) * blk, col * blk : (col + 1) * blk],
            )
            total = term if total is None else total + term
        for dest in range(dests):
            o, x = dest // side, dest % side
            at = o % 2 * half + x * (half // side) + o // 2 * few
            out_ref[dest, :, col * blk : (col + 1) * blk] = total[at : at + few].astype(BF16)


def sum_terms_kernel(in_ref, out_ref):
    total = in_ref[0].astype(F32)
    for part in range(1, in_ref.shape[0]):
        total = total + in_ref[part].astype(F32)
    out_ref[...] = total.astype(BF16)


def forward_kernel(nuw, last, core_ref, coef_ref, other_coef_ref, lad_ref, out_ref, order_ref):
    dests, packed, lanes = out_ref.shape
    padded = coef_ref.shape[1]
    few, cols = lad_ref.shape
    mus = cols // nuw // 2
    part_cols = 384
    run = part_cols // nuw
    row = row_ids(lanes)
    source = jnp.where(row < nuw * few, mod(row, few), -1)
    wide = mm(ones_where(source == lane_ids(few)), lad_ref[...])
    own = div(row, few) == mod(lane_ids(part_cols), nuw)
    collect = ones_where(div(lane_ids(part_cols), nuw) == row_ids(run))
    for part in range(cols // part_cols):
        some = wide[:, part * part_cols : (part + 1) * part_cols]
        some = jnp.where(own, some, 0.0).astype(BF16)
        some = lax.dot_general(collect, some, LANES, preferred_element_type=F32)
        order_ref[part * run : (part + 1) * run, :] = some.astype(BF16)
    fwd = None
    for other in range(2):
        coef = (other_coef_ref if other else coef_ref)[...]
        start = pl.multiple_of((core_ref[0] ^ other) * mus, mus)
        part = mm(coef.reshape(dests * padded, mus), order_ref[pl.ds(start, mus), :])
        fwd = part if fwd is None else fwd + part
    fwd = fwd.reshape(dests, padded, lanes)
    used = nuw * few
    free = lanes - used
    rest = [fwd[:, packed : packed + last, at : at + free] for at in range(0, used, free)]
    rest.append(jnp.zeros((dests, packed - len(rest) * last, free), F32))
    fwd = jnp.concatenate([fwd[:, :packed, :used], jnp.concatenate(rest, axis=1)], axis=2)
    out_ref[...] = fwd.astype(BF16)


def out_kernel(steps, few, fwd_ref, win_ref, out_hbm, out_ref, sems):
    parts, packed, lanes = fwd_ref.shape
    total, pairs, nv = out_ref.shape
    last = total - packed
    used = win_ref.shape[0] * few
    free = lanes - used
    side = pairs // few
    virt = total // steps
    win = repeated(win_ref[...], few, lanes)
    own = row_ids(few) == mod(lane_ids(lanes), few)
    fwds = []
    for x in range(side):
        fwd = None
        for block in range(parts // side):
            part = fwd_ref[block * side + x].astype(F32)
            fwd = part if fwd is None else fwd + part
        rest = [fwd[i * last : (i + 1) * last, used:] for i in range(used // free)]
        rest.append(jnp.zeros((last, free), F32))
        fwds.append(jnp.concatenate([fwd, jnp.concatenate(rest, axis=1)], axis=0))
    copies = []
    for step in range(steps):
        cut = slice(step * virt, (step + 1) * virt)
        wide = [jnp.broadcast_to(fwd[cut][:, None, :], (virt, few, lanes)) for fwd in fwds]
        wide = jnp.concatenate([jnp.where(own, part, 0.0) for part in wide], axis=1)
        wide = wide.reshape(virt * pairs, lanes).astype(BF16)
        out_ref[cut] = mm(wide, win).astype(BF16).reshape(virt, pairs, nv)
        copies.append(pltpu.make_async_copy(out_ref.at[cut], out_hbm.at[cut], sems.at[step]))
        copies[-1].start()
    for copy in copies:
        copy.wait()


def params(mib=24):
    return pltpu.CompilerParams(vmem_limit_bytes=mib * 1024 * 1024)


def swap(array, axis):
    return lax.ppermute(array, axis, [(0, 1), (1, 0)])


def turn(array, sizes):
    square = sizes["y"] * sizes["z"]
    pairs = [(one, one % square * square + one // square) for one in range(square * square)]
    return lax.ppermute(array, ("y", "z", "zh", "core"), pairs)


def exchange(array, axes):
    return lax.all_to_all(array, axes, split_axis=0, concat_axis=0, tiled=True)


def local(sizes, amplitudes, window_coef, virtual_coef, integrals, block_mask):
    pairs, virt, _ = amplitudes.shape
    nuw, nv = window_coef.shape
    nao = virtual_coef.shape[0]
    rows, cols = integrals.shape
    side = sizes["y"]
    sp = side * sizes["z"] * sizes["x"]
    op = sizes["zh"] * sizes["core"]
    few = pairs // side
    mus = nao * side // sp
    width = 128
    steps = 4
    padded, packed = -(-virt // 16) * 16, virt // 8 * 8
    amp = jnp.transpose(amplitudes, (1, 0, 2))
    coef = jnp.transpose(virtual_coef, (1, 0))
    my_core = lax.axis_index("core").reshape(1)
    smem = pl.BlockSpec(memory_space=pltpu.SMEM)
    hbm = pl.BlockSpec(memory_space=pltpu.HBM)
    vmem = pl.BlockSpec(memory_space=pltpu.VMEM)

    sent = pl.pallas_call(
        functools.partial(half_kernel, steps, few),
        in_specs=[smem, hbm, hbm, hbm],
        out_specs=vmem,
        out_shape=jax.ShapeDtypeStruct((sp, 2 * packed, width), BF16),
        scratch_shapes=[
            pltpu.VMEM((virt, pairs, nv), BF16),
            pltpu.VMEM((nuw, nv), BF16),
            pltpu.VMEM((nao // mus, virt, mus // 2), BF16),
            pltpu.VMEM((side, virt, width), F32),
            pltpu.VMEM((nao // mus, packed % 16 + 16, width), F32),
            pltpu.SemaphoreType.DMA((steps + 1 + nao // mus,)),
        ],
        compiler_params=params(54),
        name="half",
    )(my_core, amp, window_coef, coef)
    chunk = exchange(sent, ("y", "z", "x"))
    own_coef, half = pl.pallas_call(
        functools.partial(unpack_kernel, nuw * few, virt - packed),
        out_shape=[jax.ShapeDtypeStruct((sp, padded, width), BF16)] * 2,
        compiler_params=params(),
        name="unpack",
    )(chunk)
    other_coef = swap(own_coef, "core")
    flat = sizes["x"] * sizes["zh"]
    own_amp = pl.pallas_call(
        functools.partial(own_amp_kernel, nuw),
        out_shape=jax.ShapeDtypeStruct((few, mus // 2 * nuw), BF16),
        compiler_params=params(),
        name="own_amp",
    )(half, own_coef)
    ao_amp = pl.pallas_call(
        functools.partial(amp_kernel, nuw),
        in_specs=[smem, vmem, vmem, vmem],
        out_specs=vmem,
        out_shape=jax.ShapeDtypeStruct((flat, few, rows), BF16),
        compiler_params=params(),
        name="amp",
    )(my_core, half, other_coef, own_amp)
    amp_here = exchange(ao_amp, ("x", "zh")).reshape(flat * few, rows)
    amp_there = swap(amp_here, "core")

    terms = pl.pallas_call(
        functools.partial(terms_kernel, rows // block_mask.shape[0]),
        in_specs=[smem, smem, vmem, vmem, vmem],
        out_specs=vmem,
        out_shape=jax.ShapeDtypeStruct((sp, few, cols), BF16),
        scratch_shapes=[pltpu.VMEM((op * pairs, rows), BF16)],
        compiler_params=params(),
        name="terms",
    )(block_mask, my_core, amp_here, amp_there, integrals)
    pieces = exchange(terms, ("y", "z", "x"))
    ladder = pl.pallas_call(
        sum_terms_kernel,
        out_shape=jax.ShapeDtypeStruct((few, cols), BF16),
        compiler_params=params(),
        name="sum_terms",
    )(pieces)
    owned = turn(ladder, sizes)
    fwd = pl.pallas_call(
        functools.partial(forward_kernel, nuw, virt - packed),
        in_specs=[smem, vmem, vmem, vmem],
        out_specs=vmem,
        out_shape=jax.ShapeDtypeStruct((sp, packed, width), BF16),
        scratch_shapes=[pltpu.VMEM((mus, width), BF16)],
        compiler_params=params(),
        name="forward",
    )(my_core, own_coef, other_coef, owned)
    fwd = exchange(fwd, ("y", "z", "x"))
    out = pl.pallas_call(
        functools.partial(out_kernel, steps, few),
        in_specs=[vmem, vmem],
        out_specs=hbm,
        out_shape=jax.ShapeDtypeStruct((virt, pairs, nv), BF16),
        scratch_shapes=[pltpu.VMEM((virt, pairs, nv), BF16), pltpu.SemaphoreType.DMA((steps,))],
        compiler_params=params(),
        name="out",
    )(fwd, window_coef)
    return jnp.transpose(out, (1, 0, 2))


def solution(mesh):
    sizes = {"y": 4, "z": 2, "x": 4, "zh": 4, "core": 2}
    fine = Mesh(mesh.devices.reshape(tuple(sizes.values())), tuple(sizes))
    sp, op = ("y", "z", "x"), ("zh", "core")
    placed = (P(op, sp, None), P(), P(None, sp), P(sp, op), P(sp, op))
    return jax.shard_map(
        functools.partial(local, sizes),
        mesh=fine,
        in_specs=placed,
        out_specs=P(op, sp, None),
        check_vma=False,
    )
```

```python
import functools

import jax
import jax.numpy as jnp
from jax import lax
from jax.experimental import pallas as pl
from jax.experimental.pallas import tpu as pltpu
from jax.sharding import Mesh
from jax.sharding import PartitionSpec as P

F32 = jnp.float32
BF16 = jnp.bfloat16
ROWS = (((0,), (0,)), ((), ()))
LANES = (((1,), (1,)), ((), ()))


def iota(shape, dim):
    return lax.broadcasted_iota(jnp.int32, shape, dim)


def div(x, n):
    if n & (n - 1) == 0:
        return lax.shift_right_logical(x, n.bit_length() - 1)
    return lax.shift_right_logical(x * ((1 << 19) // n + 1), 19)


def mod(x, n):
    return x & (n - 1) if n & (n - 1) == 0 else x - div(x, n) * n


def row_ids(size):
    return iota((size, 1), 0)


def lane_ids(size):
    return iota((1, size), 1)


def ones_where(cond):
    return jnp.where(cond, 1.0, 0.0).astype(BF16)


def mm(x, y):
    return jnp.dot(x, y, preferred_element_type=F32)


def repeated(win, few, width):
    nuw, nv = win.shape
    win = jnp.broadcast_to(win.astype(F32)[:, None, :], (nuw, few, nv)).reshape(nuw * few, nv)
    return jnp.concatenate([win, jnp.zeros((width - nuw * few, nv), F32)], axis=0).astype(BF16)


def half_kernel(
    steps, few, core_ref, amp_hbm, win_hbm, coef_hbm, out_ref, amp_ref, win_ref, coef_ref, half_ref, rest_ref, sems
):
    total, pairs, _ = amp_hbm.shape
    dests, both, width = out_ref.shape
    blocks, _, mus = coef_ref.shape
    packed = both // 2
    side = pairs // few
    last = total - packed
    cols = win_hbm.shape[0] * few
    free = width - cols
    virt = total // steps
    rows = virt * pairs
    ahead = 3
    copies = [
        pltpu.make_async_copy(
            amp_hbm.at[step * virt : (step + 1) * virt],
            amp_ref.at[step * virt : (step + 1) * virt],
            sems.at[step],
        )
        for step in range(steps)
    ]
    win_copy = pltpu.make_async_copy(win_hbm, win_ref, sems.at[steps])
    coef_copies = []
    for b in range(blocks):
        start = pl.multiple_of((2 * b + core_ref[0]) * mus, mus)
        coef_copies.append(
            pltpu.make_async_copy(coef_hbm.at[:, pl.ds(start, mus)], coef_ref.at[b], sems.at[steps + 1 + b])
        )
    for copy in coef_copies:
        copy.start()
    win_copy.start()
    for copy in copies[:ahead]:
        copy.start()
    high = mus // free * last
    whole = packed // 16 * 16
    for b in range(blocks):
        coef_copies[b].wait()
        coef = coef_ref[b].astype(F32)
        rest = [coef[packed:, at : at + free] for at in range(0, mus, free)]
        rest = jnp.concatenate(rest, axis=0)
        rest = jnp.concatenate([jnp.zeros((high, cols), F32), rest], axis=1)
        rest_ref[b] = jnp.concatenate([coef[whole:packed], rest], axis=0)
        for x in range(side):
            out_ref[b * side + x, :whole] = coef[:whole].astype(BF16)
    win_copy.wait()
    win = repeated(win_ref[...], few, width)
    own = mod(row_ids(few), few) == mod(lane_ids(width), few)
    for step in range(steps):
        copies[step].wait()
        if step + ahead < steps:
            copies[step + ahead].start()
        block = amp_ref[step * virt : (step + 1) * virt].reshape(rows, amp_ref.shape[2])
        half = lax.dot_general(block, win, LANES, preferred_element_type=F32)
        half = half.astype(BF16).astype(F32).reshape(virt, side, few, width)
        for x in range(side):
            part = jnp.sum(jnp.where(own, half[:, x], 0.0), axis=1)
            half_ref[x, step * virt : (step + 1) * virt, :] = part
    halves = []
    for x in range(side):
        half = half_ref[x]
        rest = [jnp.zeros((mus // free * last, free), F32)]
        rest += [half[packed:, at : at + free] for at in range(0, cols, free)]
        rest.append(jnp.zeros((packed - (mus + cols) // free * last, free), F32))
        halves.append(jnp.concatenate([half[:packed, :cols], jnp.concatenate(rest, axis=0)], axis=1))
    left = packed - whole
    middle = high + left
    for x in range(side):
        low = halves[x][middle:].astype(BF16)
        for b in range(blocks):
            rest = rest_ref[b]
            piece = [rest[:left], rest[left:] + halves[x][:high], halves[x][high:middle]]
            piece = jnp.concatenate(piece, axis=0).astype(BF16)
            out_ref[b * side + x, whole : packed + middle] = piece
            out_ref[b * side + x, packed + middle :] = low


def amp_of(nuw, few, half, coef):
    depth, mus = coef.shape
    every = mus * nuw
    width = half.shape[1]
    amp = lax.dot_general(coef, half, ROWS, preferred_element_type=F32).astype(BF16)
    wide = mm(ones_where(div(row_ids(every), nuw) == lane_ids(mus)), amp)
    own = mod(row_ids(every), nuw) == div(lane_ids(width), few)
    wide = jnp.where(own, wide, 0.0).astype(BF16)
    pick = ones_where(row_ids(2 * few) == mod(lane_ids(width), few))
    return lax.dot_general(pick, wide, LANES, preferred_element_type=F32)[:few].astype(BF16)


def unpack_kernel(cols, last, in_ref, coef_ref, half_ref):
    parts, both, mus = in_ref.shape
    packed = both // 2
    free = mus - cols
    whole = in_ref[...].astype(F32)
    rest = whole[:, packed:, cols:]
    none = jnp.zeros((parts, coef_ref.shape[1] - packed - last, mus), F32)
    count = mus // free
    coef = [rest[:, i * last : (i + 1) * last] for i in range(count)]
    coef = jnp.concatenate([whole[:, :packed], jnp.concatenate(coef, axis=2), none], axis=1)
    coef_ref[...] = coef.astype(BF16)
    half = [rest[:, i * last : (i + 1) * last] for i in range(count, count + cols // free)]
    half.append(jnp.zeros((parts, last, free), F32))
    half = jnp.concatenate([whole[:, packed:], jnp.concatenate(half, axis=2), none], axis=1)
    half_ref[...] = half.astype(BF16)


def own_amp_kernel(nuw, half_ref, coef_ref, out_ref):
    parts, padded, mus = coef_ref.shape
    coef = coef_ref[...].reshape(parts * padded, mus)
    half = half_ref[...].reshape(parts * padded, mus)
    out_ref[...] = amp_of(nuw, out_ref.shape[0], half, coef)


def amp_kernel(nuw, core_ref, half_ref, coef_ref, own_ref, out_ref):
    parts, padded, mus = coef_ref.shape
    dests, few, cols = out_ref.shape
    repeat = dests * cols // (2 * mus * nuw)
    blocks = dests // (2 * repeat)
    half = half_ref[...].reshape(parts * padded, mus)
    other_amp = amp_of(nuw, few, half, coef_ref[...].reshape(parts * padded, mus))
    for other, amp in enumerate([own_ref[...], other_amp]):
        for b in range(blocks):
            for zh in range(repeat):
                dest = ((core_ref[0] ^ other) * blocks + b) * repeat + zh
                out_ref[dest] = amp[:, b * cols : (b + 1) * cols]


def terms_of(blk, mask_ref, amp_ref, ints_ref, store):
    rows, cols = ints_ref.shape
    side, few = 4, 8
    per = amp_ref.shape[0] // side
    for col in range(cols // blk):
        total = None
        for row in range(rows // blk):
            keep = mask_ref[row, col].astype(F32)
            term = keep * mm(
                amp_ref[:, row * blk : (row + 1) * blk],
                ints_ref[row * blk : (row + 1) * blk, col * blk : (col + 1) * blk],
            )
            total = term if total is None else total + term
        for x in range(side):
            for zh in range(per // few):
                at = x * per + zh * few
                store(zh, x, slice(col * blk, (col + 1) * blk), total[at : at + few].astype(BF16))


def own_terms_kernel(blk, mask_ref, amp_ref, ints_ref, out_ref):
    def store(zh, x, cut, part):
        out_ref[zh * 4 + x, :, cut] = part

    terms_of(blk, mask_ref, amp_ref, ints_ref, store)


def terms_kernel(blk, mask_ref, core_ref, amp_ref, ints_ref, own_ref, out_ref):
    side = 4
    for part in range(own_ref.shape[0]):
        zh, x = part // side, part % side
        out_ref[(zh * 2 + core_ref[0]) * side + x] = own_ref[part]

    def store(zh, x, cut, part):
        out_ref[(zh * 2 + (core_ref[0] ^ 1)) * side + x, :, cut] = part

    terms_of(blk, mask_ref, amp_ref, ints_ref, store)


def sum_terms_kernel(in_ref, out_ref):
    total = in_ref[0].astype(F32)
    for part in range(1, in_ref.shape[0]):
        total = total + in_ref[part].astype(F32)
    out_ref[...] = total.astype(BF16)


def forward_kernel(nuw, last, core_ref, coef_ref, other_coef_ref, lad_ref, out_ref, order_ref):
    dests, packed, lanes = out_ref.shape
    padded = coef_ref.shape[1]
    few, cols = lad_ref.shape
    mus = cols // nuw // 2
    part_cols = 384
    run = part_cols // nuw
    row = row_ids(lanes)
    source = jnp.where(row < nuw * few, mod(row, few), -1)
    wide = mm(ones_where(source == lane_ids(few)), lad_ref[...])
    own = div(row, few) == mod(lane_ids(part_cols), nuw)
    collect = ones_where(div(lane_ids(part_cols), nuw) == row_ids(run))
    for part in range(cols // part_cols):
        some = wide[:, part * part_cols : (part + 1) * part_cols]
        some = jnp.where(own, some, 0.0).astype(BF16)
        some = lax.dot_general(collect, some, LANES, preferred_element_type=F32)
        order_ref[part * run : (part + 1) * run, :] = some.astype(BF16)
    fwd = None
    for other in range(2):
        coef = (other_coef_ref if other else coef_ref)[...]
        start = pl.multiple_of((core_ref[0] ^ other) * mus, mus)
        part = mm(coef.reshape(dests * padded, mus), order_ref[pl.ds(start, mus), :])
        fwd = part if fwd is None else fwd + part
    fwd = fwd.reshape(dests, padded, lanes)
    used = nuw * few
    free = lanes - used
    rest = [fwd[:, packed : packed + last, at : at + free] for at in range(0, used, free)]
    rest.append(jnp.zeros((dests, packed - len(rest) * last, free), F32))
    fwd = jnp.concatenate([fwd[:, :packed, :used], jnp.concatenate(rest, axis=1)], axis=2)
    out_ref[...] = fwd.astype(BF16)


def out_kernel(steps, few, fwd_ref, win_ref, out_hbm, out_ref, sems):
    parts, packed, lanes = fwd_ref.shape
    total, pairs, nv = out_ref.shape
    last = total - packed
    used = win_ref.shape[0] * few
    free = lanes - used
    side = pairs // few
    virt = total // steps
    win = repeated(win_ref[...], few, lanes)
    own = row_ids(few) == mod(lane_ids(lanes), few)
    fwds = []
    for x in range(side):
        fwd = None
        for block in range(parts // side):
            part = fwd_ref[block * side + x].astype(F32)
            fwd = part if fwd is None else fwd + part
        rest = [fwd[i * last : (i + 1) * last, used:] for i in range(used // free)]
        rest.append(jnp.zeros((last, free), F32))
        fwds.append(jnp.concatenate([fwd, jnp.concatenate(rest, axis=1)], axis=0))
    copies = []
    for step in range(steps):
        cut = slice(step * virt, (step + 1) * virt)
        wide = [jnp.broadcast_to(fwd[cut][:, None, :], (virt, few, lanes)) for fwd in fwds]
        wide = jnp.concatenate([jnp.where(own, part, 0.0) for part in wide], axis=1)
        wide = wide.reshape(virt * pairs, lanes).astype(BF16)
        out_ref[cut] = mm(wide, win).astype(BF16).reshape(virt, pairs, nv)
        copies.append(pltpu.make_async_copy(out_ref.at[cut], out_hbm.at[cut], sems.at[step]))
        copies[-1].start()
    for copy in copies:
        copy.wait()


def params(mib=24):
    return pltpu.CompilerParams(vmem_limit_bytes=mib * 1024 * 1024)


def swap(array, axis):
    return lax.ppermute(array, axis, [(0, 1), (1, 0)])


def turn(array, sizes):
    square = sizes["y"] * sizes["z"]
    pairs = [(one, one % square * square + one // square) for one in range(square * square)]
    return lax.ppermute(array, ("y", "z", "zh", "core"), pairs)


def exchange(array, axes):
    return lax.all_to_all(array, axes, split_axis=0, concat_axis=0, tiled=True)


def local(sizes, amplitudes, window_coef, virtual_coef, integrals, block_mask):
    pairs, virt, _ = amplitudes.shape
    nuw, nv = window_coef.shape
    nao = virtual_coef.shape[0]
    rows, cols = integrals.shape
    side = sizes["y"]
    sp = side * sizes["z"] * sizes["x"]
    op = sizes["zh"] * sizes["core"]
    few = pairs // side
    mus = nao * side // sp
    width = 128
    steps = 4
    padded, packed = -(-virt // 16) * 16, virt // 8 * 8
    amp = jnp.transpose(amplitudes, (1, 0, 2))
    coef = jnp.transpose(virtual_coef, (1, 0))
    my_core = lax.axis_index("core").reshape(1)
    smem = pl.BlockSpec(memory_space=pltpu.SMEM)
    hbm = pl.BlockSpec(memory_space=pltpu.HBM)
    vmem = pl.BlockSpec(memory_space=pltpu.VMEM)

    sent = pl.pallas_call(
        functools.partial(half_kernel, steps, few),
        in_specs=[smem, hbm, hbm, hbm],
        out_specs=vmem,
        out_shape=jax.ShapeDtypeStruct((sp, 2 * packed, width), BF16),
        scratch_shapes=[
            pltpu.VMEM((virt, pairs, nv), BF16),
            pltpu.VMEM((nuw, nv), BF16),
            pltpu.VMEM((nao // mus, virt, mus // 2), BF16),
            pltpu.VMEM((side, virt, width), F32),
            pltpu.VMEM((nao // mus, packed % 16 + 16, width), F32),
            pltpu.SemaphoreType.DMA((steps + 1 + nao // mus,)),
        ],
        compiler_params=params(54),
        name="half",
    )(my_core, amp, window_coef, coef)
    chunk = exchange(sent, ("y", "z", "x"))
    own_coef, half = pl.pallas_call(
        functools.partial(unpack_kernel, nuw * few, virt - packed),
        out_shape=[jax.ShapeDtypeStruct((sp, padded, width), BF16)] * 2,
        compiler_params=params(),
        name="unpack",
    )(chunk)
    other_coef = swap(own_coef, "core")
    flat = sizes["x"] * sizes["zh"]
    own_amp = pl.pallas_call(
        functools.partial(own_amp_kernel, nuw),
        out_shape=jax.ShapeDtypeStruct((few, mus // 2 * nuw), BF16),
        compiler_params=params(),
        name="own_amp",
    )(half, own_coef)
    ao_amp = pl.pallas_call(
        functools.partial(amp_kernel, nuw),
        in_specs=[smem, vmem, vmem, vmem],
        out_specs=vmem,
        out_shape=jax.ShapeDtypeStruct((flat, few, rows), BF16),
        compiler_params=params(),
        name="amp",
    )(my_core, half, other_coef, own_amp)
    amp_here = exchange(ao_amp, ("x", "zh")).reshape(flat * few, rows)
    amp_there = swap(amp_here, "core")

    blk = rows // block_mask.shape[0]
    own_terms = pl.pallas_call(
        functools.partial(own_terms_kernel, blk),
        in_specs=[smem, vmem, vmem],
        out_specs=vmem,
        out_shape=jax.ShapeDtypeStruct((sp // 2, few, cols), BF16),
        compiler_params=params(),
        name="own_terms",
    )(block_mask, amp_here, integrals)
    terms = pl.pallas_call(
        functools.partial(terms_kernel, blk),
        in_specs=[smem, smem, vmem, vmem, vmem],
        out_specs=vmem,
        out_shape=jax.ShapeDtypeStruct((sp, few, cols), BF16),
        compiler_params=params(),
        name="terms",
    )(block_mask, my_core, amp_there, integrals, own_terms)
    pieces = exchange(terms, ("y", "z", "x"))
    ladder = pl.pallas_call(
        sum_terms_kernel,
        out_shape=jax.ShapeDtypeStruct((few, cols), BF16),
        compiler_params=params(),
        name="sum_terms",
    )(pieces)
    owned = turn(ladder, sizes)
    fwd = pl.pallas_call(
        functools.partial(forward_kernel, nuw, virt - packed),
        in_specs=[smem, vmem, vmem, vmem],
        out_specs=vmem,
        out_shape=jax.ShapeDtypeStruct((sp, packed, width), BF16),
        scratch_shapes=[pltpu.VMEM((mus, width), BF16)],
        compiler_params=params(),
        name="forward",
    )(my_core, own_coef, other_coef, owned)
    fwd = exchange(fwd, ("y", "z", "x"))
    out = pl.pallas_call(
        functools.partial(out_kernel, steps, few),
        in_specs=[vmem, vmem],
        out_specs=hbm,
        out_shape=jax.ShapeDtypeStruct((virt, pairs, nv), BF16),
        scratch_shapes=[pltpu.VMEM((virt, pairs, nv), BF16), pltpu.SemaphoreType.DMA((steps,))],
        compiler_params=params(),
        name="out",
    )(fwd, window_coef)
    return jnp.transpose(out, (1, 0, 2))


def solution(mesh):
    sizes = {"y": 4, "z": 2, "x": 4, "zh": 4, "core": 2}
    fine = Mesh(mesh.devices.reshape(tuple(sizes.values())), tuple(sizes))
    sp, op = ("y", "z", "x"), ("zh", "core")
    placed = (P(op, sp, None), P(), P(None, sp), P(sp, op), P(sp, op))
    return jax.shard_map(
        functools.partial(local, sizes),
        mesh=fine,
        in_specs=placed,
        out_specs=P(op, sp, None),
        check_vma=False,
    )
```

```python
import functools

import jax
import jax.numpy as jnp
from jax import lax
from jax.experimental import pallas as pl
from jax.experimental.pallas import tpu as pltpu
from jax.sharding import Mesh
from jax.sharding import PartitionSpec as P

F32 = jnp.float32
BF16 = jnp.bfloat16
ROWS = (((0,), (0,)), ((), ()))
LANES = (((1,), (1,)), ((), ()))


def iota(shape, dim):
    return lax.broadcasted_iota(jnp.int32, shape, dim)


def div(x, n):
    if n & (n - 1) == 0:
        return lax.shift_right_logical(x, n.bit_length() - 1)
    return lax.shift_right_logical(x * ((1 << 19) // n + 1), 19)


def mod(x, n):
    return x & (n - 1) if n & (n - 1) == 0 else x - div(x, n) * n


def row_ids(size):
    return iota((size, 1), 0)


def lane_ids(size):
    return iota((1, size), 1)


def ones_where(cond):
    return jnp.where(cond, 1.0, 0.0).astype(BF16)


def mm(x, y):
    return jnp.dot(x, y, preferred_element_type=F32)


def repeated(win, few, width):
    nuw, nv = win.shape
    win = jnp.broadcast_to(win.astype(F32)[:, None, :], (nuw, few, nv)).reshape(nuw * few, nv)
    return jnp.concatenate([win, jnp.zeros((width - nuw * few, nv), F32)], axis=0).astype(BF16)


def half_kernel(
    steps, few, core_ref, amp_hbm, win_hbm, coef_hbm, out_ref, amp_ref, win_ref, coef_ref, half_ref, rest_ref, sems
):
    total, pairs, _ = amp_hbm.shape
    dests, both, width = out_ref.shape
    blocks, _, mus = coef_ref.shape
    packed = both // 2
    side = pairs // few
    last = total - packed
    cols = win_hbm.shape[0] * few
    free = width - cols
    virt = total // steps
    rows = virt * pairs
    ahead = steps
    copies = [
        pltpu.make_async_copy(
            amp_hbm.at[step * virt : (step + 1) * virt],
            amp_ref.at[step * virt : (step + 1) * virt],
            sems.at[step],
        )
        for step in range(steps)
    ]
    win_copy = pltpu.make_async_copy(win_hbm, win_ref, sems.at[steps])
    coef_copies = []
    for b in range(blocks):
        start = pl.multiple_of((2 * b + core_ref[0]) * mus, mus)
        coef_copies.append(
            pltpu.make_async_copy(coef_hbm.at[:, pl.ds(start, mus)], coef_ref.at[b], sems.at[steps + 1 + b])
        )
    for copy in coef_copies:
        copy.start()
    win_copy.start()
    for copy in copies[:ahead]:
        copy.start()
    high = mus // free * last
    whole = packed // 16 * 16
    for b in range(blocks):
        coef_copies[b].wait()
        coef = coef_ref[b].astype(F32)
        rest = [coef[packed:, at : at + free] for at in range(0, mus, free)]
        rest = jnp.concatenate(rest, axis=0)
        rest = jnp.concatenate([jnp.zeros((high, cols), F32), rest], axis=1)
        rest_ref[b] = jnp.concatenate([coef[whole:packed], rest], axis=0)
        for x in range(side):
            out_ref[b * side + x, :whole] = coef[:whole].astype(BF16)
    win_copy.wait()
    win = repeated(win_ref[...], few, width)
    own = mod(row_ids(few), few) == mod(lane_ids(width), few)
    for step in range(steps):
        copies[step].wait()
        if step + ahead < steps:
            copies[step + ahead].start()
        block = amp_ref[step * virt : (step + 1) * virt].reshape(rows, amp_ref.shape[2])
        half = lax.dot_general(block, win, LANES, preferred_element_type=F32)
        half = half.astype(BF16).astype(F32).reshape(virt, side, few, width)
        for x in range(side):
            part = jnp.sum(jnp.where(own, half[:, x], 0.0), axis=1)
            half_ref[x, step * virt : (step + 1) * virt, :] = part
    halves = []
    for x in range(side):
        half = half_ref[x]
        rest = [jnp.zeros((mus // free * last, free), F32)]
        rest += [half[packed:, at : at + free] for at in range(0, cols, free)]
        rest.append(jnp.zeros((packed - (mus + cols) // free * last, free), F32))
        halves.append(jnp.concatenate([half[:packed, :cols], jnp.concatenate(rest, axis=0)], axis=1))
    left = packed - whole
    middle = high + left
    for x in range(side):
        low = halves[x][middle:].astype(BF16)
        for b in range(blocks):
            rest = rest_ref[b]
            piece = [rest[:left], rest[left:] + halves[x][:high], halves[x][high:middle]]
            piece = jnp.concatenate(piece, axis=0).astype(BF16)
            out_ref[b * side + x, whole : packed + middle] = piece
            out_ref[b * side + x, packed + middle :] = low


def amp_of(nuw, few, half, coef):
    depth, mus = coef.shape
    every = mus * nuw
    width = half.shape[1]
    amp = lax.dot_general(coef, half, ROWS, preferred_element_type=F32).astype(BF16)
    wide = mm(ones_where(div(row_ids(every), nuw) == lane_ids(mus)), amp)
    own = mod(row_ids(every), nuw) == div(lane_ids(width), few)
    wide = jnp.where(own, wide, 0.0).astype(BF16)
    pick = ones_where(row_ids(2 * few) == mod(lane_ids(width), few))
    return lax.dot_general(pick, wide, LANES, preferred_element_type=F32)[:few].astype(BF16)


def unpack_kernel(cols, last, half, in_ref, out_ref):
    parts, both, mus = in_ref.shape
    packed = both // 2
    free = mus - cols
    count = mus // free
    rest = in_ref[...].astype(F32)[:, packed:, cols:]
    if half:
        main = in_ref[...].astype(F32)[:, packed:]
        tail = [rest[:, i * last : (i + 1) * last] for i in range(count, count + cols // free)]
        tail.append(jnp.zeros((parts, last, free), F32))
    else:
        main = in_ref[...].astype(F32)[:, :packed]
        tail = [rest[:, i * last : (i + 1) * last] for i in range(count)]
    none = jnp.zeros((parts, out_ref.shape[1] - packed - last, mus), F32)
    out_ref[...] = jnp.concatenate([main, jnp.concatenate(tail, axis=2), none], axis=1).astype(BF16)


def own_amp_kernel(nuw, half_ref, coef_ref, out_ref):
    parts, padded, mus = coef_ref.shape
    coef = coef_ref[...].reshape(parts * padded, mus)
    half = half_ref[...].reshape(parts * padded, mus)
    out_ref[...] = amp_of(nuw, out_ref.shape[0], half, coef)


def amp_kernel(nuw, core_ref, half_ref, coef_ref, own_ref, out_ref):
    parts, padded, mus = coef_ref.shape
    dests, few, cols = out_ref.shape
    repeat = dests * cols // (2 * mus * nuw)
    blocks = dests // (2 * repeat)
    half = half_ref[...].reshape(parts * padded, mus)
    other_amp = amp_of(nuw, few, half, coef_ref[...].reshape(parts * padded, mus))
    for other, amp in enumerate([own_ref[...], other_amp]):
        for b in range(blocks):
            for zh in range(repeat):
                dest = ((core_ref[0] ^ other) * blocks + b) * repeat + zh
                out_ref[dest] = amp[:, b * cols : (b + 1) * cols]


def terms_of(blk, mask_ref, amp_ref, ints_ref, store):
    rows, cols = ints_ref.shape
    side, few = 4, 8
    per = amp_ref.shape[0] // side
    for col in range(cols // blk):
        total = None
        for row in range(rows // blk):
            keep = mask_ref[row, col].astype(F32)
            term = keep * mm(
                amp_ref[:, row * blk : (row + 1) * blk],
                ints_ref[row * blk : (row + 1) * blk, col * blk : (col + 1) * blk],
            )
            total = term if total is None else total + term
        for x in range(side):
            for zh in range(per // few):
                at = x * per + zh * few
                store(zh, x, slice(col * blk, (col + 1) * blk), total[at : at + few].astype(BF16))


def own_terms_kernel(blk, mask_ref, amp_ref, ints_ref, out_ref):
    def store(zh, x, cut, part):
        out_ref[zh * 4 + x, :, cut] = part

    terms_of(blk, mask_ref, amp_ref, ints_ref, store)


def terms_kernel(blk, mask_ref, core_ref, amp_ref, ints_ref, own_ref, out_ref):
    side = 4
    for part in range(own_ref.shape[0]):
        zh, x = part // side, part % side
        out_ref[(zh * 2 + core_ref[0]) * side + x] = own_ref[part]

    def store(zh, x, cut, part):
        out_ref[(zh * 2 + (core_ref[0] ^ 1)) * side + x, :, cut] = part

    terms_of(blk, mask_ref, amp_ref, ints_ref, store)


def sum_terms_kernel(in_ref, out_ref):
    total = in_ref[0].astype(F32)
    for part in range(1, in_ref.shape[0]):
        total = total + in_ref[part].astype(F32)
    out_ref[...] = total.astype(BF16)


def forward_kernel(nuw, last, core_ref, coef_ref, other_coef_ref, lad_ref, out_ref, order_ref):
    dests, packed, lanes = out_ref.shape
    padded = coef_ref.shape[1]
    few, cols = lad_ref.shape
    mus = cols // nuw // 2
    part_cols = 384
    run = part_cols // nuw
    row = row_ids(lanes)
    source = jnp.where(row < nuw * few, mod(row, few), -1)
    wide = mm(ones_where(source == lane_ids(few)), lad_ref[...])
    own = div(row, few) == mod(lane_ids(part_cols), nuw)
    collect = ones_where(div(lane_ids(part_cols), nuw) == row_ids(run))
    for part in range(cols // part_cols):
        some = wide[:, part * part_cols : (part + 1) * part_cols]
        some = jnp.where(own, some, 0.0).astype(BF16)
        some = lax.dot_general(collect, some, LANES, preferred_element_type=F32)
        order_ref[part * run : (part + 1) * run, :] = some.astype(BF16)
    fwd = None
    for other in range(2):
        coef = (other_coef_ref if other else coef_ref)[...]
        start = pl.multiple_of((core_ref[0] ^ other) * mus, mus)
        part = mm(coef.reshape(dests * padded, mus), order_ref[pl.ds(start, mus), :])
        fwd = part if fwd is None else fwd + part
    fwd = fwd.reshape(dests, padded, lanes)
    used = nuw * few
    free = lanes - used
    rest = [fwd[:, packed : packed + last, at : at + free] for at in range(0, used, free)]
    rest.append(jnp.zeros((dests, packed - len(rest) * last, free), F32))
    fwd = jnp.concatenate([fwd[:, :packed, :used], jnp.concatenate(rest, axis=1)], axis=2)
    out_ref[...] = fwd.astype(BF16)


def out_kernel(steps, few, fwd_ref, win_ref, out_hbm, out_ref, sems):
    parts, packed, lanes = fwd_ref.shape
    total, pairs, nv = out_ref.shape
    last = total - packed
    used = win_ref.shape[0] * few
    free = lanes - used
    side = pairs // few
    virt = total // steps
    win = repeated(win_ref[...], few, lanes)
    own = row_ids(few) == mod(lane_ids(lanes), few)
    fwds = []
    for x in range(side):
        fwd = None
        for block in range(parts // side):
            part = fwd_ref[block * side + x].astype(F32)
            fwd = part if fwd is None else fwd + part
        rest = [fwd[i * last : (i + 1) * last, used:] for i in range(used // free)]
        rest.append(jnp.zeros((last, free), F32))
        fwds.append(jnp.concatenate([fwd, jnp.concatenate(rest, axis=1)], axis=0))
    copies = []
    for step in range(steps):
        cut = slice(step * virt, (step + 1) * virt)
        wide = [jnp.broadcast_to(fwd[cut][:, None, :], (virt, few, lanes)) for fwd in fwds]
        wide = jnp.concatenate([jnp.where(own, part, 0.0) for part in wide], axis=1)
        wide = wide.reshape(virt * pairs, lanes).astype(BF16)
        out_ref[cut] = mm(wide, win).astype(BF16).reshape(virt, pairs, nv)
        copies.append(pltpu.make_async_copy(out_ref.at[cut], out_hbm.at[cut], sems.at[step]))
        copies[-1].start()
    for copy in copies:
        copy.wait()


def params(mib=24):
    return pltpu.CompilerParams(vmem_limit_bytes=mib * 1024 * 1024)


def swap(array, axis):
    return lax.ppermute(array, axis, [(0, 1), (1, 0)])


def turn(array, sizes):
    square = sizes["y"] * sizes["z"]
    pairs = [(one, one % square * square + one // square) for one in range(square * square)]
    return lax.ppermute(array, ("y", "z", "zh", "core"), pairs)


def exchange(array, axes):
    return lax.all_to_all(array, axes, split_axis=0, concat_axis=0, tiled=True)


def local(sizes, amplitudes, window_coef, virtual_coef, integrals, block_mask):
    pairs, virt, _ = amplitudes.shape
    nuw, nv = window_coef.shape
    nao = virtual_coef.shape[0]
    rows, cols = integrals.shape
    side = sizes["y"]
    sp = side * sizes["z"] * sizes["x"]
    op = sizes["zh"] * sizes["core"]
    few = pairs // side
    mus = nao * side // sp
    width = 128
    steps = 4
    padded, packed = -(-virt // 16) * 16, virt // 8 * 8
    amp = jnp.transpose(amplitudes, (1, 0, 2))
    coef = jnp.transpose(virtual_coef, (1, 0))
    my_core = lax.axis_index("core").reshape(1)
    smem = pl.BlockSpec(memory_space=pltpu.SMEM)
    hbm = pl.BlockSpec(memory_space=pltpu.HBM)
    vmem = pl.BlockSpec(memory_space=pltpu.VMEM)

    sent = pl.pallas_call(
        functools.partial(half_kernel, steps, few),
        in_specs=[smem, hbm, hbm, hbm],
        out_specs=vmem,
        out_shape=jax.ShapeDtypeStruct((sp, 2 * packed, width), BF16),
        scratch_shapes=[
            pltpu.VMEM((virt, pairs, nv), BF16),
            pltpu.VMEM((nuw, nv), BF16),
            pltpu.VMEM((nao // mus, virt, mus // 2), BF16),
            pltpu.VMEM((side, virt, width), F32),
            pltpu.VMEM((nao // mus, packed % 16 + 16, width), F32),
            pltpu.SemaphoreType.DMA((steps + 1 + nao // mus,)),
        ],
        compiler_params=params(54),
        name="half",
    )(my_core, amp, window_coef, coef)
    chunk = exchange(sent, ("y", "z", "x"))
    own_coef, half = [
        pl.pallas_call(
            functools.partial(unpack_kernel, nuw * few, virt - packed, which),
            out_shape=jax.ShapeDtypeStruct((sp, padded, width), BF16),
            compiler_params=params(),
            name="unpack",
        )(chunk)
        for which in (False, True)
    ]
    other_coef = swap(own_coef, "core")
    flat = sizes["x"] * sizes["zh"]
    own_amp = pl.pallas_call(
        functools.partial(own_amp_kernel, nuw),
        out_shape=jax.ShapeDtypeStruct((few, mus // 2 * nuw), BF16),
        compiler_params=params(),
        name="own_amp",
    )(half, own_coef)
    ao_amp = pl.pallas_call(
        functools.partial(amp_kernel, nuw),
        in_specs=[smem, vmem, vmem, vmem],
        out_specs=vmem,
        out_shape=jax.ShapeDtypeStruct((flat, few, rows), BF16),
        compiler_params=params(),
        name="amp",
    )(my_core, half, other_coef, own_amp)
    amp_here = exchange(ao_amp, ("x", "zh")).reshape(flat * few, rows)
    amp_there = swap(amp_here, "core")

    blk = rows // block_mask.shape[0]
    own_terms = pl.pallas_call(
        functools.partial(own_terms_kernel, blk),
        in_specs=[smem, vmem, vmem],
        out_specs=vmem,
        out_shape=jax.ShapeDtypeStruct((sp // 2, few, cols), BF16),
        compiler_params=params(),
        name="own_terms",
    )(block_mask, amp_here, integrals)
    terms = pl.pallas_call(
        functools.partial(terms_kernel, blk),
        in_specs=[smem, smem, vmem, vmem, vmem],
        out_specs=vmem,
        out_shape=jax.ShapeDtypeStruct((sp, few, cols), BF16),
        compiler_params=params(),
        name="terms",
    )(block_mask, my_core, amp_there, integrals, own_terms)
    pieces = exchange(terms, ("y", "z", "x"))
    ladder = pl.pallas_call(
        sum_terms_kernel,
        out_shape=jax.ShapeDtypeStruct((few, cols), BF16),
        compiler_params=params(),
        name="sum_terms",
    )(pieces)
    owned = turn(ladder, sizes)
    fwd = pl.pallas_call(
        functools.partial(forward_kernel, nuw, virt - packed),
        in_specs=[smem, vmem, vmem, vmem],
        out_specs=vmem,
        out_shape=jax.ShapeDtypeStruct((sp, packed, width), BF16),
        scratch_shapes=[pltpu.VMEM((mus, width), BF16)],
        compiler_params=params(),
        name="forward",
    )(my_core, own_coef, other_coef, owned)
    fwd = exchange(fwd, ("y", "z", "x"))
    out = pl.pallas_call(
        functools.partial(out_kernel, steps, few),
        in_specs=[vmem, vmem],
        out_specs=hbm,
        out_shape=jax.ShapeDtypeStruct((virt, pairs, nv), BF16),
        scratch_shapes=[pltpu.VMEM((virt, pairs, nv), BF16), pltpu.SemaphoreType.DMA((steps,))],
        compiler_params=params(),
        name="out",
    )(fwd, window_coef)
    return jnp.transpose(out, (1, 0, 2))


def solution(mesh):
    sizes = {"y": 4, "z": 2, "x": 4, "zh": 4, "core": 2}
    fine = Mesh(mesh.devices.reshape(tuple(sizes.values())), tuple(sizes))
    sp, op = ("y", "z", "x"), ("zh", "core")
    placed = (P(op, sp, None), P(), P(None, sp), P(sp, op), P(sp, op))
    return jax.shard_map(
        functools.partial(local, sizes),
        mesh=fine,
        in_specs=placed,
        out_specs=P(op, sp, None),
        check_vma=False,
    )
```
